512 devices in a mesh: dp: 4 (over y), gx: 4 (over z_hi), gy: 4 (over z_lo), gz: 8 (over x, core).
Axes of the slice: x: 4, y: 4, z: 16 (z_hi: 4, z_lo: 4; z = z_hi * 4 + z_lo), core: 2. Of those that a mesh axis runs over, the one named last changes fastest.
Arguments:
- inputs: bfloat16 [12288, 4096], P(('dp', 'gx', 'gz'), 'gy'), may hold values from -0.5 to 0.5
- out_grad: bfloat16 [12288, 14336], P(('dp', 'gx', 'gy'), 'gz'), may hold values from -6 to 6
- weight: bfloat16 [4096, 14336], P(('gy', 'gx'), 'gz'), may hold values from -0.09375 to 0.09375
Outputs:
- input_grad: bfloat16 [12288, 4096], P(('dp', 'gx', 'gz'), 'gy')
- weight_grad: bfloat16 [4096, 14336], P(('gy', 'gx'), 'gz')
The draws below stay inside these ranges and needn't reach their ends.
All inputs are finite; a program needn't handle non-finite values.
Results may differ from the reference program's by a relative error of at most 0.017.
Values may be sent and summed in bfloat16 or wider, within the bound.
A program may use at most 64 MiB of HBM per device.

```python
import jax
import jax.numpy as jnp
from jax import lax

D = 4096
FF = 14336
TOK_DEV = 768
TOKENS = 12288
N_DP = 4
N_GX = 4
N_GZ = 8


def block_levels(stream_key, extent, split, smallest, largest):
    level, own = 1.0, jax.random.fold_in(stream_key, 6)
    for dim, shards_of in split:
        heights = jnp.exp(jax.random.uniform(jax.random.fold_in(own, dim), (shards_of,), jnp.float32, smallest / len(split), largest / len(split)))
        level = level * jnp.repeat(heights, extent[dim] // shards_of).reshape([-1 if axis == dim else 1 for axis in range(len(extent))])
    return level


def gaussian(rng, extent, deviation, reach, cuts=(), held_as=jnp.bfloat16):
    result = jax.random.normal(rng, extent, jnp.float32) * deviation
    if len(cuts) > 0:
        result = block_levels(rng, extent, cuts, -0.22, 0.18) * result
    return jnp.clip(result, min=-reach, max=reach).astype(held_as)


def setup_inputs(seed: int = 0) -> dict:
    key_list = jax.random.split(jax.random.key(seed), 4)
    inputs = gaussian(key_list[0], (TOKENS, D), (N_DP * (TOK_DEV * N_DP * N_GX) ** -0.5), 0.5, ((0, 128), (1, 4)))
    out_grad = gaussian(key_list[1], (TOKENS, FF), 1.0, 6.0, ((0, 64), (1, 8)))
    weight = gaussian(key_list[2], (D, FF), D ** -0.5, 0.09375, ((0, 16), (1, 8)))
    return {"inputs": inputs, "out_grad": out_grad, "weight": weight}


def reference(inputs, out_grad, weight):
    blocks = N_DP * N_GX
    input_blocks = inputs.reshape(blocks, TOK_DEV, D)
    grad_blocks = out_grad.reshape(blocks, TOK_DEV, FF)

    def add_block(total, pair):
        left, right = pair
        term = jnp.dot(left.T, right, preferred_element_type=jnp.float32).astype(jnp.bfloat16)
        term = lax.optimization_barrier(term)
        return total + term.astype(jnp.float32), None

    total, _ = lax.scan(add_block, jnp.zeros((D, FF), jnp.float32), (input_blocks, grad_blocks))
    weight_grad = (total / N_DP).astype(jnp.bfloat16)

    width = FF // N_GZ
    grad_cols = out_grad.reshape(TOKENS, N_GZ, width).transpose(1, 0, 2)
    weight_cols = weight.reshape(D, N_GZ, width).transpose(1, 0, 2)

    def add_cols(total, pair):
        left, right = pair
        term = jnp.dot(left, right.T, preferred_element_type=jnp.float32).astype(jnp.bfloat16)
        term = lax.optimization_barrier(term)
        return total + term.astype(jnp.float32), None

    summed, _ = lax.scan(add_cols, jnp.zeros((TOKENS, D), jnp.float32), (grad_cols, weight_cols))
    input_grad = summed.astype(jnp.bfloat16)
    return input_grad, weight_grad
```

```python
import jax
import jax.numpy as jnp
from jax import lax
from jax.sharding import PartitionSpec as P


def per_device(inputs, out_grad, weight):
    groups = lax.axis_size("dp")
    blocks = lax.axis_size("gx")
    width = inputs.shape[1]
    rows, hidden = weight.shape
    part = rows // groups

    own = lax.dynamic_slice_in_dim(weight, lax.axis_index("dp") * part, part, 0)
    own = lax.all_gather(own, "gx", axis=0, tiled=False)
    whole = lax.all_gather(own, "dp", axis=1, tiled=False).reshape(width, hidden)
    grad_rows = lax.all_gather(out_grad, "gy", axis=0, tiled=True)
    total = lax.dot_general(
        lax.all_gather(inputs, "gz", axis=0, tiled=True),
        grad_rows,
        (((0,), (0,)), ((), ())),
        preferred_element_type=jnp.float32,
    )
    rounded = total.astype(jnp.bfloat16).reshape(blocks, groups, part, hidden)
    summed = lax.psum_scatter(rounded, "dp", scatter_dimension=1, tiled=False)
    summed = lax.psum_scatter(summed, "gx", scatter_dimension=0, tiled=False)
    summed = (summed.astype(jnp.float32) / groups).astype(jnp.bfloat16)
    weight_grad = lax.all_gather(summed, "dp", axis=0, tiled=True)

    terms = lax.dot_general(
        grad_rows,
        whole,
        (((1,), (1,)), ((), ())),
        preferred_element_type=jnp.float32,
    )
    input_grad = lax.psum_scatter(terms.astype(jnp.bfloat16), "gz", scatter_dimension=0, tiled=True)
    return (input_grad, weight_grad)


def solution(mesh):
    return jax.shard_map(
        per_device,
        mesh=mesh,
        in_specs=(P(("dp", "gx", "gz"), "gy"), P(("dp", "gx", "gy"), "gz"), P(("gy", "gx"), "gz")),
        out_specs=(P(("dp", "gx", "gz"), "gy"), P(("gy", "gx"), "gz")),
        check_vma=False,
    )
```

```python
import functools

import jax
import jax.numpy as jnp
from jax import lax
from jax.experimental import pallas as pl
from jax.experimental.pallas import tpu as pltpu
from jax.sharding import PartitionSpec as P

MESH = pl.DeviceIdType.MESH
NC = 8
HOP = 2
START = 12
BF16, F32 = jnp.bfloat16, jnp.float32


def kernel(
    inp, og, wt, ig_out, wg_out,
    G, W, X, I1, PT, RD, T, CT, S, XR, R, Q, O, FB,
    wr, ws, dr, dss, yr, ysd, gr, gs, g2r, g2s, s1r, s1s, s2r, s2s, s3r, s3s, s4r, s4s,
    ctr, cts, xrr, xrs, qr, qs, orr, ors, loc,
):
    y, h, zl = lax.axis_index("dp"), lax.axis_index("gx"), lax.axis_index("gy")
    gz = lax.axis_index("gz")
    x, c = gz // 2, gz % 2
    z = h * 4 + zl
    r = (zl - y + 4) % 4
    tok = og.shape[0] // 2
    half = 4 * tok
    quarter = inp.shape[1] // 4
    rows = wt.shape[0] // NC

    def zdev(zz):
        return {"gx": zz // 4, "gy": zz % 4}

    def xdev(xx):
        return {"gz": xx * 2 + c}

    right = (zdev((z + 1) % 16), zdev((z + 15) % 16))
    ydev = ({"dp": (y + 1) % 4}, {"dp": (y + 3) % 4})
    core = {"gz": x * 2 + 1 - c}
    rd = (r, (4 - r) % 4)
    rr = tuple(jnp.where(v == 0, 4, v) for v in rd)
    sign = (1, -1)

    def held_from(d, cls):
        return ((z - sign[d] * (rd[d] + 4 * cls) + 32) % 16) // 4

    def bound_for(d, s):
        return ((z + sign[d] * (4 - rd[d] + 4 * (1 - s)) + 32) % 16) // 4

    def in_half(d, i):
        return i < NC // 2 if d == 0 else i >= NC // 2

    def remote(src, dst, send, recv, dev):
        return pltpu.make_async_remote_copy(
            src_ref=src, dst_ref=dst, send_sem=send, recv_sem=recv, device_id=dev, device_id_type=MESH
        )

    def tokens(first):
        return pl.ds(pl.multiple_of(first, 32), tok)

    def halves(which):
        return pl.ds(pl.multiple_of(which * half, 128), half)

    def chunk(i):
        return pl.ds(pl.multiple_of(i * rows, rows), rows)

    def columns(q):
        return pl.ds(pl.multiple_of(q * quarter, 128), quarter)

    def w_copy(d, stream, i):
        part = W.at[held_from(d, stream), chunk(i)]
        return remote(part, part, ws.at[d, stream, i], wr.at[d, stream, i], right[d])

    def d_copy(d, s, i):
        to = s + jnp.where(rd[d] == 3, 1, 0)
        return remote(RD.at[d, s, chunk(i)], RD.at[d, to, chunk(i)], dss.at[d, s, i], dr.at[d, s, i], right[d])

    def y_copy(d, i):
        return remote(FB.at[chunk(i)], FB.at[chunk(i)], ysd.at[d, i], yr.at[i], ydev[d])

    def g_copy(d, k):
        part = G.at[tokens(k * half + y * tok)]
        return remote(part, part, gs.at[d, k], gr.at[d, k], ydev[d])

    def g2_copy(d):
        part = G.at[tokens(d * half + ((y + 3 + 2 * d) % 4) * tok)]
        return remote(part, part, g2s.at[d], g2r.at[d], ydev[d])

    def s1_copy(dx):
        to = (x + dx) % 4
        return remote(inp.at[:, columns(to)], I1.at[x], s1s.at[dx], s1r.at[x], xdev(to))

    def s2_copy(t):
        j = (zl + t) % 4
        return remote(I1.at[j], X.at[x, tokens(c * half + y * tok)], s2s.at[t], s2r.at[y], {"dp": zl, "gy": j})

    def s3_copy(dx):
        part = X.at[x, halves(c)]
        return remote(part, part, s3s.at[dx], s3r.at[x], xdev((x + dx) % 4))

    def s4_copy(g):
        part = X.at[g, halves(c)]
        return remote(part, part, s4s.at[g], s4r.at[g], core)

    def ct_copy(g):
        return remote(T.at[g, halves(1 - c)], CT.at[g], cts.at[g], ctr.at[g], core)

    def xr_copy(dx):
        to = (x + dx) % 4
        return remote(S.at[to], XR.at[x], xrs.at[dx], xrr.at[x], xdev(to))

    def q_copy(t):
        k = (y + t) % 4
        return remote(R.at[tokens(k * tok)], Q.at[zl], qs.at[t], qr.at[zl], {"dp": k, "gy": y})

    def o_copy(dx):
        to = (x + dx) % 4
        return remote(Q.at[to], O.at[x], ors.at[dx], orr.at[x], xdev(to))

    def arrived(dst, send, recv, dev):
        remote(dst, dst, send, recv, dev).wait_recv()

    barrier = pltpu.get_barrier_semaphore()

    def greet(dev):
        pl.semaphore_signal(barrier, inc=1, device_id=dev, device_id_type=MESH)

    for dev in (*right, *ydev, core):
        greet(dev)
    for dx in (1, 2, 3):
        greet(xdev((x + dx) % 4))
    for t in (1, 2, 3):
        greet({"dp": zl, "gy": (zl + t) % 4})
        greet({"dp": (y + t) % 4, "gy": y})

    @pl.when(r != 0)
    def _():
        greet({"dp": zl, "gy": zl})
        greet({"dp": y, "gy": y})

    own = [
        pltpu.make_async_copy(og.at[pl.ds(k * tok, tok)], G.at[tokens(k * half + y * tok)], loc.at[k]) for k in (0, 1)
    ]
    own.append(pltpu.make_async_copy(inp.at[:, columns(x)], I1.at[x], loc.at[2]))
    for copy in own:
        copy.start()

    @pl.when(r == 0)
    def _():
        held = pltpu.make_async_copy(wt, W.at[h], loc.at[3])
        held.start()
        held.wait()

    for copy in own:
        copy.wait()
    pl.semaphore_wait(barrier, jnp.where(r == 0, 14, 16))

    for dx in (1, 2, 3):
        s1_copy(dx).start()
    for k in (0, 1):
        g_copy(0, k).start()
        g_copy(1, 1 - k).start()

    @pl.when(r == 0)
    def _():
        def first(i, _):
            w_copy(0, 0, i).start()
            w_copy(1, 0, i).start()
            return 0

        lax.fori_loop(0, NC, first, 0)

    def w_step(d, s):
        m = s - HOP * rr[d]

        @pl.when((m >= 0) & (m < 2 * NC))
        def _():
            stream, i = m // NC, m % NC
            cls = stream + jnp.where(rd[d] == 0, 1, 0)

            @pl.when((cls < 2) | in_half(d, i))
            def _():
                part = W.at[held_from(d, cls), chunk(i)]
                arrived(part, ws.at[d, 0, 0], wr.at[d, stream, i], right[d])

            @pl.when((cls == 0) | ((cls == 1) & ((rd[d] != 3) | in_half(d, i))))
            def _():
                w_copy(d, cls, i).start()

    def add(d, s, i, received):
        own_term = PT[bound_for(d, s), chunk(i), :]
        if received:
            own_term = own_term + RD[d, s, chunk(i), :].astype(F32)
        RD[d, s, chunk(i), :] = own_term.astype(BF16)
        d_copy(d, s, i).start()

    def d_step(d, s):
        @pl.when((rd[d] == 0) & (s >= 0) & (s < NC))
        def _():
            @pl.when(in_half(d, s))
            def _():
                add(d, 0, s, False)

        m = s - HOP * rr[d]

        @pl.when((m >= 0) & (m < 2 * NC))
        def _():
            stream, i = m // NC, m % NC
            slot = stream + jnp.where(rd[d] == 0, 1, 0)
            expected = (slot > 0) | (rd[d] > 1) | in_half(d, i)

            @pl.when(expected)
            def _():
                arrived(RD.at[d, slot, chunk(i)], dss.at[d, 0, 0], dr.at[d, stream, i], right[d])

            @pl.when((slot < 2) & expected)
            def _():
                add(d, slot, i, True)

            @pl.when((slot < 2) & jnp.logical_not(expected))
            def _():
                add(d, slot, i, False)

    groups = 4

    def last_step(s):
        i = s - HOP * 4 - NC

        @pl.when((r == 0) & (i >= 0) & (i < NC))
        def _():
            total = PT[h, chunk(i), :] + RD[0, 2, chunk(i), :].astype(F32) + RD[1, 2, chunk(i), :].astype(F32)
            mean = (total / groups).astype(BF16)
            FB[chunk(i), :] = mean
            wg_out[chunk(i), :] = mean
            y_copy(0, i).start()
            y_copy(1, i).start()

        away = rd[1]
        n = i - HOP * jnp.where(away == 2, 2, 1)

        @pl.when((r != 0) & (n >= 0) & (n < NC))
        def _():
            arrived(FB.at[chunk(n)], ysd.at[0, 0], yr.at[n], ydev[0])

            @pl.when((away == 1) & (n % 2 == 0))
            def _():
                y_copy(0, n).start()

            @pl.when((away == 3) & (n % 2 == 1))
            def _():
                y_copy(1, n).start()

            wg_out[chunk(n), :] = FB[chunk(n), :]

    def in_places():
        for dx in (1, 2, 3):
            j = (x + dx) % 4
            arrived(I1.at[j], s1s.at[0], s1r.at[j], core)

        @pl.when(r == 0)
        def _():
            mine = pltpu.make_async_copy(I1.at[zl], X.at[x, tokens(c * half + y * tok)], loc.at[3])
            mine.start()
            mine.wait()

        @pl.when(r != 0)
        def _():
            s2_copy(0).start()

        for t in (1, 2, 3):
            s2_copy(t).start()

    def grad_relay():
        for d in (0, 1):
            k = (y + 3 + 2 * d) % 4
            arrived(G.at[tokens(d * half + k * tok)], gs.at[0, 0], gr.at[d, d], core)
            g2_copy(d).start()

    def in_spread():
        for t in (0, 1, 2, 3):
            k = (y + t) % 4

            def wait(k=k):
                arrived(X.at[x, tokens(c * half + k * tok)], s2s.at[0], s2r.at[k], core)

            if t == 0:
                pl.when(r != 0)(wait)
            else:
                wait()
        for dx in (1, 2, 3):
            s3_copy(dx).start()
        s4_copy(x).start()

    def in_cores():
        for dx in (1, 2, 3):
            g = (x + dx) % 4
            arrived(X.at[g, halves(c)], s3s.at[0], s3r.at[g], core)
            s4_copy(g).start()

    def in_done():
        for g in range(4):
            arrived(X.at[g, halves(1 - c)], s4s.at[0], s4r.at[g], core)
        for d in (0, 1):
            k = (y + 3 + 2 * d) % 4
            arrived(G.at[tokens((1 - d) * half + k * tok)], gs.at[0, 0], gr.at[d, 1 - d], core)
            k = (y + 2) % 4
            arrived(G.at[tokens(d * half + k * tok)], g2s.at[0], g2r.at[d], core)

    def p_job(g):
        def tile(n, _):
            cols = pl.ds(pl.multiple_of(n * 256, 256), 256)
            PT[g, :, cols] = lax.dot_general(
                X[g], G[:, cols], (((0,), (0,)), ((), ())), preferred_element_type=F32
            )
            return 0

        lax.fori_loop(0, G.shape[1] // 256, tile, 0)

    def t_job(g):
        def part(n, _):
            where = halves((1 - c + n) % 2)
            T[g, where, :] = lax.dot_general(
                G[where, :], W[g], (((1,), (1,)), ((), ())), preferred_element_type=F32
            ).astype(BF16)

            @pl.when(n == 0)
            def _():
                ct_copy(g).start()

            return 0

        lax.fori_loop(0, 2, part, 0)

    def cores_sum(g):
        arrived(CT.at[g], cts.at[0], ctr.at[g], core)
        S[g] = (T[g, halves(c), :].astype(F32) + CT[g].astype(F32)).astype(BF16)

    def x_send():
        for g in range(4):
            cores_sum(g)
        for dx in (1, 2, 3):
            xr_copy(dx).start()

    def x_sum():
        total = S[x].astype(F32)
        for dx in (1, 2, 3):
            g = (x + dx) % 4
            arrived(XR.at[g], xrs.at[0], xrr.at[g], core)
            total = total + XR[g].astype(F32)
        R[...] = total.astype(BF16)

        @pl.when(r == 0)
        def _():
            mine = pltpu.make_async_copy(R.at[tokens(y * tok)], Q.at[zl], loc.at[3])
            mine.start()
            mine.wait()

        @pl.when(r != 0)
        def _():
            q_copy(0).start()

        for t in (1, 2, 3):
            q_copy(t).start()

    def out_spread():
        for t in (0, 1, 2, 3):
            j = (zl + t) % 4

            def wait(j=j):
                arrived(Q.at[j], qs.at[0], qr.at[j], core)

            if t == 0:
                pl.when(r != 0)(wait)
            else:
                wait()
        for dx in (1, 2, 3):
            o_copy(dx).start()
        O[x] = Q[x]

    def out_done():
        for dx in (1, 2, 3):
            g = (x + dx) % 4
            arrived(O.at[g], ors.at[0], orr.at[g], core)
        for g in range(4):
            ig_out[:, g * quarter : (g + 1) * quarter] = O[g]

    p_jobs = (
        bound_for(0, 0),
        jnp.where(r == 0, h, bound_for(1, 0)),
        bound_for(0, 1),
        bound_for(1, 1),
    )
    t_jobs = (
        held_from(0, 0),
        jnp.where(r == 0, held_from(0, 1), held_from(1, 0)),
        jnp.where(r == 0, held_from(1, 1), held_from(0, 1)),
        jnp.where(r == 0, held_from(0, 2), held_from(1, 1)),
    )
    late = 2 * NC + 4 * HOP

    def pick(s, pairs, jobs):
        g = jobs[0]
        for at, job in zip(pairs[1:], jobs[1:], strict=True):
            g = jnp.where(s == at, job, g)
        return g

    p_at = (START, START + 1, START + 3, START + 4)
    t_at = (START + 6, START + 8, late - 1, late + 1)

    def step(s, _):
        for d in (0, 1):
            w_step(d, s)
        for at, job in ((1, in_places), (4, in_spread), (5, grad_relay), (8, in_cores), (START, in_done)):
            pl.when(s == at)(job)

        @pl.when(functools.reduce(jnp.logical_or, [s == at for at in p_at]))
        def _():
            p_job(pick(s, p_at, p_jobs))

        for d in (0, 1):
            d_step(d, s - START - 2)
        last_step(s - START - 2)

        @pl.when(functools.reduce(jnp.logical_or, [s == at for at in t_at]))
        def _():
            t_job(pick(s, t_at, t_jobs))

        for at, job in ((late + 2, x_send), (late + 6, x_sum), (late + 9, out_spread)):
            pl.when(s == at)(job)
        return 0

    lax.fori_loop(0, START + 2 + 2 * NC + 6 * HOP, step, 0)
    out_done()

    def leave(i, _):
        for d in (0, 1):
            w_copy(d, 0, i).wait_send()
            d_copy(d, 1, i).wait_send()

            @pl.when((rd[d] != 3) | in_half(d, i))
            def _(d=d):
                w_copy(d, 1, i).wait_send()

            @pl.when((rd[d] != 0) | in_half(d, i))
            def _(d=d):
                d_copy(d, 0, i).wait_send()

            @pl.when((r == 0) | ((rd[1] == 1 + 2 * d) & (i % 2 == d)))
            def _(d=d):
                y_copy(d, i).wait_send()

        return 0

    lax.fori_loop(0, NC, leave, 0)
    for d in (0, 1):
        for k in (0, 1):
            g_copy(d, k).wait_send()
        g2_copy(d).wait_send()
    for n in (1, 2, 3):
        for copy in (s1_copy, s2_copy, s3_copy, xr_copy, q_copy, o_copy):
            copy(n).wait_send()

    @pl.when(r != 0)
    def _():
        s2_copy(0).wait_send()
        q_copy(0).wait_send()

    for g in range(4):
        s4_copy(g).wait_send()
        ct_copy(g).wait_send()


def per_device(inputs, out_grad, weight):
    tok, width = inputs.shape
    rows, hidden = weight.shape
    quarter = width // 4
    sems = pltpu.SemaphoreType.DMA
    vmem = pl.BlockSpec(memory_space=pltpu.VMEM)
    return pl.pallas_call(
        kernel,
        out_shape=(
            jax.ShapeDtypeStruct((tok, width), BF16),
            jax.ShapeDtypeStruct((rows, hidden), BF16),
        ),
        in_specs=[vmem] * 3,
        out_specs=(vmem, vmem),
        scratch_shapes=[
            pltpu.VMEM((8 * tok, hidden), BF16),
            pltpu.VMEM((4, rows, hidden), BF16),
            pltpu.VMEM((4, 8 * tok, quarter), BF16),
            pltpu.VMEM((4, tok, quarter), BF16),
            pltpu.VMEM((4, rows, hidden), F32),
            pltpu.VMEM((2, 3, rows, hidden), BF16),
            pltpu.VMEM((4, 8 * tok, quarter), BF16),
            pltpu.VMEM((4, 4 * tok, quarter), BF16),
            pltpu.VMEM((4, 4 * tok, quarter), BF16),
            pltpu.VMEM((4, 4 * tok, quarter), BF16),
            pltpu.VMEM((4 * tok, quarter), BF16),
            pltpu.VMEM((4, tok, quarter), BF16),
            pltpu.VMEM((4, tok, quarter), BF16),
            pltpu.VMEM((rows, hidden), BF16),
            sems((2, 2, NC)), sems((2, 2, NC)), sems((2, 2, NC)), sems((2, 2, NC)),
            sems((NC,)), sems((2, NC)),
            sems((2, 2)), sems((2, 2)), sems((2,)), sems((2,)),
            *[sems((4,)) for _ in range(16)],
            sems((4,)),
        ],
        compiler_params=pltpu.CompilerParams(
            collective_id=0, has_side_effects=True, vmem_limit_bytes=56 * 2**20
        ),
        cost_estimate=pl.CostEstimate(
            flops=4 * 8 * tok * width * hidden, bytes_accessed=4 * 2**20, transcendentals=0
        ),
        name="backward",
    )(inputs, out_grad, weight)


def solution(mesh):
    return jax.shard_map(
        per_device,
        mesh=mesh,
        in_specs=(P(("dp", "gx", "gz"), "gy"), P(("dp", "gx", "gy"), "gz"), P(("gy", "gx"), "gz")),
        out_specs=(P(("dp", "gx", "gz"), "gy"), P(("gy", "gx"), "gz")),
        check_vma=False,
    )
```

```python
import functools

import jax
import jax.numpy as jnp
from jax import lax
from jax.experimental import pallas as pl
from jax.experimental.pallas import tpu as pltpu
from jax.sharding import PartitionSpec as P

MESH = pl.DeviceIdType.MESH
NC = 8
UNIT = NC // 8
AHEAD = 1
HOP = 2
START = 12
BF16, F32 = jnp.bfloat16, jnp.float32


def kernel(
    inp, og, wt, O, wg_out,
    G, W, X, I1, I2, PT, RD, T, CT, S, XR, R, Q1, Q, FB,
    wr, ws, dr, dss, yr, ysd, gr, gs, g2r, g2s, s1r, s1s, s2r, s2s, s3r, s3s, s4r, s4s, s5r, s5s,
    ctr, cts, xrr, xrs, qr, qs, q1r, q1s, orr, ors, loc,
):
    y, h, zl = lax.axis_index("dp"), lax.axis_index("gx"), lax.axis_index("gy")
    gz = lax.axis_index("gz")
    x, c = gz // 2, gz % 2
    z = h * 4 + zl
    r = (zl - y + 4) % 4
    tok = og.shape[0] // 2
    half = 4 * tok
    quarter = inp.shape[1] // 4
    rows = wt.shape[0] // NC

    def zdev(zz):
        return {"gx": zz // 4, "gy": zz % 4}

    def xdev(xx):
        return {"gz": xx * 2 + c}

    right = (zdev((z + 1) % 16), zdev((z + 15) % 16))
    ydev = ({"dp": (y + 1) % 4}, {"dp": (y + 3) % 4})
    core = {"gz": x * 2 + 1 - c}
    rd = (r, (4 - r) % 4)
    rr = tuple(jnp.where(v == 0, 4, v) for v in rd)
    sign = (1, -1)

    def held_from(d, cls):
        return ((z - sign[d] * (rd[d] + 4 * cls) + 32) % 16) // 4

    def bound_for(d, s):
        return ((z + sign[d] * (4 - rd[d] + 4 * (1 - s)) + 32) % 16) // 4

    def in_half(d, i):
        return i < NC // 2 if d == 0 else i >= NC // 2

    def remote(src, dst, send, recv, dev):
        return pltpu.make_async_remote_copy(
            src_ref=src, dst_ref=dst, send_sem=send, recv_sem=recv, device_id=dev, device_id_type=MESH
        )

    def tokens(first):
        return pl.ds(pl.multiple_of(first, 32), tok)

    def halves(which):
        return pl.ds(pl.multiple_of(which * half, 128), half)

    def chunk(i):
        return pl.ds(pl.multiple_of(i * rows, rows), rows)

    def columns(q):
        return pl.ds(pl.multiple_of(q * quarter, 128), quarter)

    def w_copy(d, stream, i):
        part = W.at[held_from(d, stream), chunk(i)]
        return remote(part, part, ws.at[d, stream, i], wr.at[d, stream, i], right[d])

    def d_copy(d, s, i):
        to = s + jnp.where(rd[d] == 3, 1, 0)
        return remote(RD.at[d, s, chunk(i)], RD.at[d, to, chunk(i)], dss.at[d, s, i], dr.at[d, s, i], right[d])

    def y_copy(d, i):
        return remote(FB.at[chunk(i)], FB.at[chunk(i)], ysd.at[d, i], yr.at[i], ydev[d])

    def g_copy(d, k):
        part = G.at[tokens(k * half + y * tok)]
        return remote(part, part, gs.at[d, k], gr.at[d, k], ydev[d])

    def g2_copy(d):
        part = G.at[tokens(d * half + ((y + 3 + 2 * d) % 4) * tok)]
        return remote(part, part, g2s.at[d], g2r.at[d], ydev[d])

    def s1_copy(dx):
        to = (x + dx) % 4
        return remote(inp.at[:, columns(to)], I1.at[x], s1s.at[dx], s1r.at[x], xdev(to))

    def s2_copy(t):
        to = (zl + t) % 4
        return remote(I1.at[to], I2.at[zl], s2s.at[t], s2r.at[zl], {"gy": to})

    def s5_copy(t):
        to = (y + t) % 4
        return remote(I2.at[to], X.at[x, tokens(c * half + y * tok)], s5s.at[t], s5r.at[y], {"dp": to})

    def s3_copy(dx):
        part = X.at[x, halves(c)]
        return remote(part, part, s3s.at[dx], s3r.at[x], xdev((x + dx) % 4))

    def s4_copy(g):
        part = X.at[g, halves(c)]
        return remote(part, part, s4s.at[g], s4r.at[g], core)

    def ct_copy(g):
        return remote(T.at[g, halves(1 - c)], CT.at[g], cts.at[g], ctr.at[g], core)

    def xr_copy(dx):
        to = (x + dx) % 4
        return remote(S.at[to], XR.at[x], xrs.at[dx], xrr.at[x], xdev(to))

    def q1_copy(t):
        to = (y + t) % 4
        return remote(R.at[tokens(to * tok)], Q1.at[y], q1s.at[t], q1r.at[y], {"dp": to})

    def q_copy(t):
        to = (zl + t) % 4
        return remote(Q1.at[to], Q.at[zl], qs.at[t], qr.at[zl], {"gy": to})

    def o_copy(dx):
        to = (x + dx) % 4
        return remote(Q.at[to], O.at[x], ors.at[dx], orr.at[x], xdev(to))

    def arrived(dst, send, recv, dev):
        remote(dst, dst, send, recv, dev).wait_recv()

    barrier = pltpu.get_barrier_semaphore()

    def greet(dev):
        pl.semaphore_signal(barrier, inc=1, device_id=dev, device_id_type=MESH)

    for dev in (*right, core):
        greet(dev)
    for t in (1, 2, 3):
        greet(xdev((x + t) % 4))
        greet({"dp": (y + t) % 4})
        greet({"gy": (zl + t) % 4})
    own = [
        pltpu.make_async_copy(og.at[pl.ds(k * tok, tok)], G.at[tokens(k * half + y * tok)], loc.at[k]) for k in (0, 1)
    ]
    own.append(pltpu.make_async_copy(inp.at[:, columns(x)], I1.at[x], loc.at[2]))
    for copy in own:
        copy.start()

    @pl.when(r == 0)
    def _():
        held = pltpu.make_async_copy(wt, W.at[h], loc.at[3])
        held.start()
        held.wait()

    for copy in own:
        copy.wait()
    pl.semaphore_wait(barrier, 12)
    for dx in (1, 2, 3):
        s1_copy(dx).start()
    for d in (0, 1):
        g_copy(d, d).start()

    def w_own(i):
        @pl.when((r == 0) & (i < NC))
        def _():
            w_copy(0, 0, i).start()
            w_copy(1, 0, i).start()

    for i in range(AHEAD):
        w_own(i)

    def w_step(d, s):
        m = s - HOP * rr[d]

        @pl.when((m >= 0) & (m < 2 * NC))
        def _():
            stream, i = m // NC, m % NC
            cls = stream + jnp.where(rd[d] == 0, 1, 0)

            @pl.when((cls < 2) | in_half(d, i))
            def _():
                part = W.at[held_from(d, cls), chunk(i)]
                arrived(part, ws.at[d, 0, 0], wr.at[d, stream, i], right[d])

            @pl.when((cls == 0) | ((cls == 1) & ((rd[d] != 3) | in_half(d, i))))
            def _():
                w_copy(d, cls, i).start()

    def add(d, s, i, received):
        own_term = PT[bound_for(d, s), chunk(i), :]
        if received:
            own_term = own_term + RD[d, s, chunk(i), :].astype(F32)
        RD[d, s, chunk(i), :] = own_term.astype(BF16)
        d_copy(d, s, i).start()

    def d_step(d, s):
        @pl.when((rd[d] == 0) & (s >= 0) & (s < NC))
        def _():
            @pl.when(in_half(d, s))
            def _():
                add(d, 0, s, False)

        m = s - HOP * rr[d]

        @pl.when((m >= 0) & (m < 2 * NC))
        def _():
            stream, i = m // NC, m % NC
            slot = stream + jnp.where(rd[d] == 0, 1, 0)
            expected = (slot > 0) | (rd[d] > 1) | in_half(d, i)

            @pl.when(expected)
            def _():
                arrived(RD.at[d, slot, chunk(i)], dss.at[d, 0, 0], dr.at[d, stream, i], right[d])

            @pl.when((slot < 2) & expected)
            def _():
                add(d, slot, i, True)

            @pl.when((slot < 2) & jnp.logical_not(expected))
            def _():
                add(d, slot, i, False)

    groups = 4

    def last_step(s):
        i = s - HOP * 4 - NC

        @pl.when((r == 0) & (i >= 0) & (i < NC))
        def _():
            total = PT[h, chunk(i), :] + RD[0, 2, chunk(i), :].astype(F32) + RD[1, 2, chunk(i), :].astype(F32)
            mean = (total / groups).astype(BF16)
            FB[chunk(i), :] = mean
            y_copy(0, i).start()
            y_copy(1, i).start()

        away = rd[1]
        n = i - HOP * jnp.where(away == 2, 2, 1)

        @pl.when((r != 0) & (n >= 0) & (n < NC))
        def _():
            arrived(FB.at[chunk(n)], ysd.at[0, 0], yr.at[n], ydev[0])

            @pl.when((away == 1) & (n % 2 == 0))
            def _():
                y_copy(0, n).start()

            @pl.when((away == 3) & (n % 2 == 1))
            def _():
                y_copy(1, n).start()

    def in_places():
        for dx in (1, 2, 3):
            j = (x + dx) % 4
            arrived(I1.at[j], s1s.at[0], s1r.at[j], core)

        for t in (1, 2, 3):
            s2_copy(t).start()
        I2[zl] = I1[zl]

    def in_columns():
        for t in (1, 2, 3):
            j = (zl + t) % 4
            arrived(I2.at[j], s2s.at[0], s2r.at[j], core)
        for t in (1, 2, 3):
            s5_copy(t).start()
        for d in (0, 1):
            g_copy(d, 1 - d).start()
        X[x, tokens(c * half + y * tok), :] = I2[y]

    def grad_relay():
        for d in (0, 1):
            k = (y + 3 + 2 * d) % 4
            arrived(G.at[tokens(d * half + k * tok)], gs.at[0, 0], gr.at[d, d], core)
            g2_copy(d).start()

    def in_spread():
        for t in (1, 2, 3):
            k = (y + t) % 4
            arrived(X.at[x, tokens(c * half + k * tok)], s5s.at[0], s5r.at[k], core)
        for dx in (1, 2, 3):
            s3_copy(dx).start()
        s4_copy(x).start()

    def in_cores():
        for dx in (1, 2, 3):
            g = (x + dx) % 4
            arrived(X.at[g, halves(c)], s3s.at[0], s3r.at[g], core)
            s4_copy(g).start()

    def in_done():
        for g in range(4):
            arrived(X.at[g, halves(1 - c)], s4s.at[0], s4r.at[g], core)
        for d in (0, 1):
            k = (y + 3 + 2 * d) % 4
            arrived(G.at[tokens((1 - d) * half + k * tok)], gs.at[0, 0], gr.at[d, 1 - d], core)
            k = (y + 2) % 4
            arrived(G.at[tokens(d * half + k * tok)], g2s.at[0], g2r.at[d], core)

    def p_job(g):
        def tile(n, _):
            cols = pl.ds(pl.multiple_of(n * 256, 256), 256)
            PT[g, :, cols] = lax.dot_general(
                X[g], G[:, cols], (((0,), (0,)), ((), ())), preferred_element_type=F32
            )
            return 0

        lax.fori_loop(0, G.shape[1] // 256, tile, 0)

    def t_job(g, n):
        where = halves((1 - c + n) % 2)
        T[g, where, :] = lax.dot_general(
            G[where, :], W[g], (((1,), (1,)), ((), ())), preferred_element_type=F32
        ).astype(BF16)

        @pl.when(n == 0)
        def _():
            ct_copy(g).start()

    def cores_sum(g):
        arrived(CT.at[g], cts.at[0], ctr.at[g], core)
        S[g] = (T[g, halves(c), :].astype(F32) + CT[g].astype(F32)).astype(BF16)

    def x_send():
        for g in range(4):
            cores_sum(g)
        for dx in (1, 2, 3):
            xr_copy(dx).start()

    def x_sum():
        total = S[x].astype(F32)
        for dx in (1, 2, 3):
            g = (x + dx) % 4
            arrived(XR.at[g], xrs.at[0], xrr.at[g], core)
            total = total + XR[g].astype(F32)
        R[...] = total.astype(BF16)

        for t in (1, 2, 3):
            q1_copy(t).start()
        Q1[y] = R[tokens(y * tok), :]

    def out_planes():
        for t in (1, 2, 3):
            f = (y + t) % 4
            arrived(Q1.at[f], q1s.at[0], q1r.at[f], core)
        for t in (1, 2, 3):
            q_copy(t).start()
        Q[zl] = Q1[zl]

    def out_spread():
        for t in (1, 2, 3):
            j = (zl + t) % 4
            arrived(Q.at[j], qs.at[0], qr.at[j], core)
        for dx in (1, 2, 3):
            o_copy(dx).start()
        pltpu.make_async_copy(Q.at[x], O.at[x], loc.at[0]).start()

    def out_done():
        pltpu.make_async_copy(FB, wg_out, loc.at[1]).start()
        for dx in (1, 2, 3):
            g = (x + dx) % 4
            arrived(O.at[g], ors.at[0], orr.at[g], core)
        pltpu.make_async_copy(Q.at[x], O.at[x], loc.at[0]).wait()
        pltpu.make_async_copy(FB, wg_out, loc.at[1]).wait()


    p_jobs = (
        bound_for(0, 0),
        jnp.where(r == 0, h, bound_for(1, 0)),
        bound_for(0, 1),
        bound_for(1, 1),
    )
    t_jobs = (
        held_from(0, 0),
        jnp.where(r == 0, held_from(0, 1), held_from(1, 0)),
        jnp.where(r == 0, held_from(1, 1), held_from(0, 1)),
        jnp.where(r == 0, held_from(0, 2), held_from(1, 1)),
    )
    late = 2 * NC + 4 * HOP

    def pick(s, pairs, jobs):
        g = jobs[0]
        for at, job in zip(pairs[1:], jobs[1:], strict=True):
            g = jnp.where(s == at, job, g)
        return g

    p_at = (START, START + 1, START + 2 + UNIT, START + 2 + 2 * UNIT)
    t_at = (*(START + 3 * UNIT + k for k in range(4)), *(late - 1 + k for k in range(4)))

    def step(s, _):
        w_own(s + AHEAD)
        for d in (0, 1):
            w_step(d, s)
        for at, job in (
            (UNIT, in_places), (3 * UNIT, in_columns), (4 * UNIT, grad_relay),
            (5 * UNIT, in_spread), (9 * UNIT, in_cores), (START, in_done),
        ):
            pl.when(s == at)(job)

        @pl.when(functools.reduce(jnp.logical_or, [s == at for at in p_at]))
        def _():
            p_job(pick(s, p_at, p_jobs))

        for d in (0, 1):
            d_step(d, s - START - 2)
        last_step(s - START - 2)

        @pl.when(functools.reduce(jnp.logical_or, [s == at for at in t_at]))
        def _():
            n = functools.reduce(jnp.logical_or, [s == at for at in t_at[1::2]]).astype(jnp.int32)
            t_job(pick(s, t_at, [g for g in t_jobs for _ in (0, 1)]), n)

        for at, job in (
            (late + 3, x_send), (late + 3 + 3 * UNIT, x_sum), (late + 3 + 5 * UNIT, out_planes),
            (late + 3 + 7 * UNIT, out_spread),
        ):
            pl.when(s == at)(job)
        return 0

    lax.fori_loop(0, START + 2 + 2 * NC + 6 * HOP, step, 0)
    out_done()

    def leave(i, _):
        for d in (0, 1):
            w_copy(d, 0, i).wait_send()
            d_copy(d, 1, i).wait_send()

            @pl.when((rd[d] != 3) | in_half(d, i))
            def _(d=d):
                w_copy(d, 1, i).wait_send()

            @pl.when((rd[d] != 0) | in_half(d, i))
            def _(d=d):
                d_copy(d, 0, i).wait_send()

        @pl.when(r == 0)
        def _():
            y_copy(0, i).wait_send()
            y_copy(1, i).wait_send()

        @pl.when((rd[1] == 1) & (i % 2 == 0))
        def _():
            y_copy(0, i).wait_send()

        @pl.when((rd[1] == 3) & (i % 2 == 1))
        def _():
            y_copy(1, i).wait_send()

        return 0

    lax.fori_loop(0, NC, leave, 0)
    for d in (0, 1):
        for k in (0, 1):
            g_copy(d, k).wait_send()
        g2_copy(d).wait_send()
    for n in (1, 2, 3):
        for copy in (s1_copy, s2_copy, s5_copy, s3_copy, xr_copy, q1_copy, q_copy, o_copy):
            copy(n).wait_send()

    for g in range(4):
        s4_copy(g).wait_send()
        ct_copy(g).wait_send()


def place(parts, shard, ig_out, wg_out):
    count, _, quarter = parts.shape
    for g in range(count):
        ig_out[:, g * quarter : (g + 1) * quarter] = parts[g]
    wg_out[...] = shard[...]


def per_device(inputs, out_grad, weight):
    tok, width = inputs.shape
    rows, hidden = weight.shape
    quarter = width // 4
    sems = pltpu.SemaphoreType.DMA
    vmem = pl.BlockSpec(memory_space=pltpu.VMEM)
    hbm = pl.BlockSpec(memory_space=pl.ANY)
    parts, weight_grad = pl.pallas_call(
        kernel,
        out_shape=(
            jax.ShapeDtypeStruct((4, tok, quarter), BF16),
            jax.ShapeDtypeStruct((rows, hidden), BF16),
        ),
        in_specs=[hbm] * 3,
        out_specs=(hbm, hbm),
        scratch_shapes=[
            pltpu.VMEM((8 * tok, hidden), BF16),
            pltpu.VMEM((4, rows, hidden), BF16),
            pltpu.VMEM((4, 8 * tok, quarter), BF16),
            pltpu.VMEM((4, tok, quarter), BF16),
            pltpu.VMEM((4, tok, quarter), BF16),
            pltpu.VMEM((4, rows, hidden), F32),
            pltpu.VMEM((2, 3, rows, hidden), BF16),
            pltpu.VMEM((4, 8 * tok, quarter), BF16),
            pltpu.VMEM((4, 4 * tok, quarter), BF16),
            pltpu.VMEM((4, 4 * tok, quarter), BF16),
            pltpu.VMEM((4, 4 * tok, quarter), BF16),
            pltpu.VMEM((4 * tok, quarter), BF16),
            pltpu.VMEM((4, tok, quarter), BF16),
            pltpu.VMEM((4, tok, quarter), BF16),
            pltpu.VMEM((rows, hidden), BF16),
            sems((2, 2, NC)), sems((2, 2, NC)), sems((2, 2, NC)), sems((2, 2, NC)),
            sems((NC,)), sems((2, NC)),
            sems((2, 2)), sems((2, 2)), sems((2,)), sems((2,)),
            *[sems((4,)) for _ in range(20)],
            sems((4,)),
        ],
        compiler_params=pltpu.CompilerParams(
            collective_id=0, has_side_effects=True, vmem_limit_bytes=56 * 2**20
        ),
        cost_estimate=pl.CostEstimate(
            flops=4 * 8 * tok * width * hidden, bytes_accessed=4 * 2**20, transcendentals=0
        ),
        name="backward",
    )(inputs, out_grad, weight)
    return pl.pallas_call(
        place,
        out_shape=(
            jax.ShapeDtypeStruct((tok, width), BF16),
            jax.ShapeDtypeStruct((rows, hidden), BF16),
        ),
        in_specs=[vmem] * 2,
        out_specs=(vmem, vmem),
        name="place",
    )(parts, weight_grad)


def solution(mesh):
    return jax.shard_map(
        per_device,
        mesh=mesh,
        in_specs=(P(("dp", "gx", "gz"), "gy"), P(("dp", "gx", "gy"), "gz"), P(("gy", "gx"), "gz")),
        out_specs=(P(("dp", "gx", "gz"), "gy"), P(("gy", "gx"), "gz")),
        check_vma=False,
    )
```

```python
import functools

import jax
import jax.numpy as jnp
from jax import lax
from jax.experimental import pallas as pl
from jax.experimental.pallas import tpu as pltpu
from jax.sharding import PartitionSpec as P

MESH = pl.DeviceIdType.MESH
NC = 8
UNIT = NC // 8
AHEAD = 1
LEAD = 2
HOP = 2
START = 12
BF16, F32 = jnp.bfloat16, jnp.float32


def kernel(
    inp, og, wt, O, wg_out,
    G, W, X, I1, I2, PT, RD, T, CT, S, XR, R, Q1, Q, FB,
    wr, ws, dr, dss, yr, ysd, y2r, y2s, kept, gr, gs, g2r, g2s, s1r, s1s, s2r, s2s, s3r, s3s, s4r, s4s, s5r, s5s,
    ctr, cts, xrr, xrs, qr, qs, q1r, q1s, orr, ors, loc,
):
    y, h, zl = lax.axis_index("dp"), lax.axis_index("gx"), lax.axis_index("gy")
    gz = lax.axis_index("gz")
    x, c = gz // 2, gz % 2
    z = h * 4 + zl
    r = (zl - y + 4) % 4
    tok = og.shape[0] // 2
    half = 4 * tok
    quarter = inp.shape[1] // 4
    rows = wt.shape[0] // NC

    def zdev(zz):
        return {"gx": zz // 4, "gy": zz % 4}

    def xdev(xx):
        return {"gz": xx * 2 + c}

    right = (zdev((z + 1) % 16), zdev((z + 15) % 16))
    ydev = ({"dp": (y + 1) % 4}, {"dp": (y + 3) % 4})
    core = {"gz": x * 2 + 1 - c}
    rd = (r, (4 - r) % 4)
    rr = tuple(jnp.where(v == 0, 4, v) for v in rd)
    sign = (1, -1)

    def held_from(d, cls):
        return ((z - sign[d] * (rd[d] + 4 * cls) + 32) % 16) // 4

    def bound_for(d, s):
        return ((z + sign[d] * (4 - rd[d] + 4 * (1 - s)) + 32) % 16) // 4

    def in_half(d, i):
        return i < NC // 2 if d == 0 else i >= NC // 2

    def remote(src, dst, send, recv, dev):
        return pltpu.make_async_remote_copy(
            src_ref=src, dst_ref=dst, send_sem=send, recv_sem=recv, device_id=dev, device_id_type=MESH
        )

    def tokens(first):
        return pl.ds(pl.multiple_of(first, 32), tok)

    def halves(which):
        return pl.ds(pl.multiple_of(which * half, 128), half)

    def chunk(i):
        return pl.ds(pl.multiple_of(i * rows, rows), rows)

    def chunk_half(i, d):
        return pl.ds(pl.multiple_of(i * rows + d * (rows // 2), rows // 2), rows // 2)

    def columns(q):
        return pl.ds(pl.multiple_of(q * quarter, 128), quarter)

    def w_copy(d, stream, i):
        part = W.at[held_from(d, stream), chunk(i)]
        return remote(part, part, ws.at[d, stream, i], wr.at[d, stream, i], right[d])

    def d_copy(d, s, i):
        to = s + jnp.where(rd[d] == 3, 1, 0)
        return remote(RD.at[d, s, chunk(i)], RD.at[d, to, chunk(i)], dss.at[d, s, i], dr.at[d, s, i], right[d])

    def y_copy(d, i):
        return remote(FB.at[chunk(i)], FB.at[chunk(i)], ysd.at[d, i], yr.at[i], ydev[d])

    def y2_copy(d, i):
        part = FB.at[chunk_half(i, d)]
        return remote(part, part, y2s.at[d, i], y2r.at[d, i], ydev[d])

    def stored(i):
        return pltpu.make_async_copy(FB.at[chunk(i)], wg_out.at[chunk(i)], kept.at[i])

    def g_copy(d, k):
        part = G.at[tokens(k * half + y * tok)]
        return remote(part, part, gs.at[d, k], gr.at[d, k], ydev[d])

    def g2_copy(d):
        part = G.at[tokens(d * half + ((y + 3 + 2 * d) % 4) * tok)]
        return remote(part, part, g2s.at[d], g2r.at[d], ydev[d])

    def s1_copy(dx):
        to = (x + dx) % 4
        return remote(inp.at[:, columns(to)], I1.at[x], s1s.at[dx], s1r.at[x], xdev(to))

    def s2_copy(t):
        to = (zl + t) % 4
        return remote(I1.at[to], I2.at[zl], s2s.at[t], s2r.at[zl], {"gy": to})

    def s5_copy(t):
        to = (y + t) % 4
        return remote(I2.at[to], X.at[x, tokens(c * half + y * tok)], s5s.at[t], s5r.at[y], {"dp": to})

    def s3_copy(dx):
        part = X.at[x, halves(c)]
        return remote(part, part, s3s.at[dx], s3r.at[x], xdev((x + dx) % 4))

    def s4_copy(g):
        part = X.at[g, halves(c)]
        return remote(part, part, s4s.at[g], s4r.at[g], core)

    def ct_copy(g):
        return remote(T.at[g, halves(1 - c)], CT.at[g], cts.at[g], ctr.at[g], core)

    def xr_copy(dx):
        to = (x + dx) % 4
        return remote(S.at[to], XR.at[x], xrs.at[dx], xrr.at[x], xdev(to))

    def q1_copy(t):
        to = (y + t) % 4
        return remote(R.at[tokens(to * tok)], Q1.at[y], q1s.at[t], q1r.at[y], {"dp": to})

    def q_copy(t):
        to = (zl + t) % 4
        return remote(Q1.at[to], Q.at[zl], qs.at[t], qr.at[zl], {"gy": to})

    def o_copy(dx):
        to = (x + dx) % 4
        return remote(Q.at[to], O.at[x], ors.at[dx], orr.at[x], xdev(to))

    def arrived(dst, send, recv, dev):
        remote(dst, dst, send, recv, dev).wait_recv()

    barrier = pltpu.get_barrier_semaphore()

    def greet(dev):
        pl.semaphore_signal(barrier, inc=1, device_id=dev, device_id_type=MESH)

    for dev in (*right, core):
        greet(dev)
    for t in (1, 2, 3):
        greet(xdev((x + t) % 4))
        greet({"dp": (y + t) % 4})
        greet({"gy": (zl + t) % 4})
    own = [
        pltpu.make_async_copy(og.at[pl.ds(k * tok, tok)], G.at[tokens(k * half + y * tok)], loc.at[k]) for k in (0, 1)
    ]
    own.append(pltpu.make_async_copy(inp.at[:, columns(x)], I1.at[x], loc.at[2]))
    for copy in own:
        copy.start()

    @pl.when(r == 0)
    def _():
        held = pltpu.make_async_copy(wt, W.at[h], loc.at[3])
        held.start()
        held.wait()

    pl.semaphore_wait(barrier, 12)
    for dx in (1, 2, 3):
        s1_copy(dx).start()
    for copy in own:
        copy.wait()
    for d in (0, 1):
        g_copy(d, d).start()

    def w_own(i):
        @pl.when((r == 0) & (i < NC))
        def _():
            w_copy(0, 0, i).start()
            w_copy(1, 0, i).start()

    for i in range(AHEAD):
        w_own(i)

    def w_step(d, s):
        m = s - HOP * rr[d]

        @pl.when((m >= 0) & (m < 2 * NC))
        def _():
            stream, i = m // NC, m % NC
            cls = stream + jnp.where(rd[d] == 0, 1, 0)

            @pl.when((cls < 2) | in_half(d, i))
            def _():
                part = W.at[held_from(d, cls), chunk(i)]
                arrived(part, ws.at[d, 0, 0], wr.at[d, stream, i], right[d])

            @pl.when((cls == 0) | ((cls == 1) & ((rd[d] != 3) | in_half(d, i))))
            def _():
                w_copy(d, cls, i).start()

    def add(d, s, i, received):
        own_term = PT[bound_for(d, s), chunk(i), :]
        if received:
            own_term = own_term + RD[d, s, chunk(i), :].astype(F32)
        RD[d, s, chunk(i), :] = own_term.astype(BF16)
        d_copy(d, s, i).start()

    def d_step(d, s):
        @pl.when((rd[d] == 0) & (s >= 0) & (s < NC))
        def _():
            @pl.when(in_half(d, s))
            def _():
                add(d, 0, s, False)

        m = s - HOP * rr[d]

        @pl.when((m >= 0) & (m < 2 * NC))
        def _():
            stream, i = m // NC, m % NC
            slot = stream + jnp.where(rd[d] == 0, 1, 0)
            expected = (slot > 0) | (rd[d] > 1) | in_half(d, i)

            @pl.when(expected)
            def _():
                arrived(RD.at[d, slot, chunk(i)], dss.at[d, 0, 0], dr.at[d, stream, i], right[d])

            @pl.when((slot < 2) & expected)
            def _():
                add(d, slot, i, True)

            @pl.when((slot < 2) & jnp.logical_not(expected))
            def _():
                add(d, slot, i, False)

    groups = 4

    def last_step(s):
        i = s - HOP * 4 - NC

        @pl.when((r == 0) & (i >= 0) & (i < NC))
        def _():
            total = PT[h, chunk(i), :] + RD[0, 2, chunk(i), :].astype(F32) + RD[1, 2, chunk(i), :].astype(F32)
            mean = (total / groups).astype(BF16)
            FB[chunk(i), :] = mean
            y_copy(0, i).start()
            y_copy(1, i).start()
            stored(i).start()

        away = rd[1]
        n = i - HOP * jnp.where(away == 2, 2, 1)

        @pl.when((r != 0) & (n >= 0) & (n < NC))
        def _():
            @pl.when(away != 2)
            def _():
                arrived(FB.at[chunk(n)], ysd.at[0, 0], yr.at[n], ydev[0])

            @pl.when(away == 1)
            def _():
                y2_copy(0, n).start()

            @pl.when(away == 3)
            def _():
                y2_copy(1, n).start()

            @pl.when(away == 2)
            def _():
                for d in (0, 1):
                    arrived(FB.at[chunk_half(n, d)], y2s.at[0, 0], y2r.at[d, n], ydev[0])

            stored(n).start()

    def in_places():
        for dx in (1, 2, 3):
            j = (x + dx) % 4
            arrived(I1.at[j], s1s.at[0], s1r.at[j], core)

        for t in (1, 2, 3):
            s2_copy(t).start()
        I2[zl] = I1[zl]

    def in_columns():
        for t in (1, 2, 3):
            j = (zl + t) % 4
            arrived(I2.at[j], s2s.at[0], s2r.at[j], core)
        for t in (1, 2, 3):
            s5_copy(t).start()
        for d in (0, 1):
            g_copy(d, 1 - d).start()
        X[x, tokens(c * half + y * tok), :] = I2[y]

    def grad_relay():
        for d in (0, 1):
            k = (y + 3 + 2 * d) % 4
            arrived(G.at[tokens(d * half + k * tok)], gs.at[0, 0], gr.at[d, d], core)
            g2_copy(d).start()

    def in_spread():
        for t in (1, 2, 3):
            k = (y + t) % 4
            arrived(X.at[x, tokens(c * half + k * tok)], s5s.at[0], s5r.at[k], core)
        for dx in (1, 2, 3):
            s3_copy(dx).start()
        s4_copy(x).start()

    def in_cores():
        for dx in (1, 2, 3):
            g = (x + dx) % 4
            arrived(X.at[g, halves(c)], s3s.at[0], s3r.at[g], core)
            s4_copy(g).start()

    def in_done():
        for g in range(4):
            arrived(X.at[g, halves(1 - c)], s4s.at[0], s4r.at[g], core)
        for d in (0, 1):
            k = (y + 3 + 2 * d) % 4
            arrived(G.at[tokens((1 - d) * half + k * tok)], gs.at[0, 0], gr.at[d, 1 - d], core)
            k = (y + 2) % 4
            arrived(G.at[tokens(d * half + k * tok)], g2s.at[0], g2r.at[d], core)

    def p_job(g):
        def tile(n, _):
            cols = pl.ds(pl.multiple_of(n * 256, 256), 256)
            PT[g, :, cols] = lax.dot_general(
                X[g], G[:, cols], (((0,), (0,)), ((), ())), preferred_element_type=F32
            )
            return 0

        lax.fori_loop(0, G.shape[1] // 256, tile, 0)

    def t_job(g, n):
        where = halves((1 - c + n) % 2)
        T[g, where, :] = lax.dot_general(
            G[where, :], W[g], (((1,), (1,)), ((), ())), preferred_element_type=F32
        ).astype(BF16)

        @pl.when(n == 0)
        def _():
            ct_copy(g).start()

    def cores_sum(g):
        arrived(CT.at[g], cts.at[0], ctr.at[g], core)
        S[g] = (T[g, halves(c), :].astype(F32) + CT[g].astype(F32)).astype(BF16)

    def x_send():
        for g in range(4):
            cores_sum(g)
        for dx in (1, 2, 3):
            xr_copy(dx).start()

    def x_sum():
        total = S[x].astype(F32)
        for dx in (1, 2, 3):
            g = (x + dx) % 4
            arrived(XR.at[g], xrs.at[0], xrr.at[g], core)
            total = total + XR[g].astype(F32)
        R[...] = total.astype(BF16)

        for t in (1, 2, 3):
            q1_copy(t).start()
        Q1[y] = R[tokens(y * tok), :]

    def out_planes():
        for t in (1, 2, 3):
            f = (y + t) % 4
            arrived(Q1.at[f], q1s.at[0], q1r.at[f], core)
        for t in (1, 2, 3):
            q_copy(t).start()
        Q[zl] = Q1[zl]

    def out_spread():
        for t in (1, 2, 3):
            j = (zl + t) % 4
            arrived(Q.at[j], qs.at[0], qr.at[j], core)
        for dx in (1, 2, 3):
            o_copy(dx).start()
        pltpu.make_async_copy(Q.at[x], O.at[x], loc.at[0]).start()

    def out_done():
        for dx in (1, 2, 3):
            g = (x + dx) % 4
            arrived(O.at[g], ors.at[0], orr.at[g], core)
        pltpu.make_async_copy(Q.at[x], O.at[x], loc.at[0]).wait()

    p_jobs = (
        bound_for(0, 0),
        jnp.where(r == 0, h, bound_for(1, 0)),
        bound_for(0, 1),
        bound_for(1, 1),
    )
    t_jobs = (
        held_from(0, 0),
        jnp.where(r == 0, held_from(0, 1), held_from(1, 0)),
        jnp.where(r == 0, held_from(1, 1), held_from(0, 1)),
        jnp.where(r == 0, held_from(0, 2), held_from(1, 1)),
    )
    late = 2 * NC + 4 * HOP

    def pick(s, pairs, jobs):
        g = jobs[0]
        for at, job in zip(pairs[1:], jobs[1:], strict=True):
            g = jnp.where(s == at, job, g)
        return g

    p_at = (START, START + 1, START + 2 + UNIT, START + 2 + 2 * UNIT)
    t_at = (*(START + 3 * UNIT + k for k in range(4)), *(late - 1 + k for k in range(4)))

    def step(s, _):
        w_own(s + AHEAD)
        for d in (0, 1):
            w_step(d, s)
        for at, job in (
            (UNIT, in_places), (3 * UNIT, in_columns), (4 * UNIT, grad_relay),
            (5 * UNIT, in_spread), (9 * UNIT, in_cores), (START, in_done),
        ):
            pl.when(s == at)(job)

        @pl.when(functools.reduce(jnp.logical_or, [s == at for at in p_at]))
        def _():
            p_job(pick(s, p_at, p_jobs))

        for d in (0, 1):
            d_step(d, s - START - LEAD)
        last_step(s - START - LEAD)

        @pl.when(functools.reduce(jnp.logical_or, [s == at for at in t_at]))
        def _():
            n = functools.reduce(jnp.logical_or, [s == at for at in t_at[1::2]]).astype(jnp.int32)
            t_job(pick(s, t_at, [g for g in t_jobs for _ in (0, 1)]), n)

        for at, job in (
            (late + 3, x_send), (late + 3 + 3 * UNIT, x_sum), (late + 3 + 5 * UNIT, out_planes),
            (late + 3 + 7 * UNIT, out_spread),
        ):
            pl.when(s == at)(job)
        return 0

    lax.fori_loop(0, START + LEAD + 2 * NC + 6 * HOP, step, 0)
    out_done()

    def leave(i, _):
        for d in (0, 1):
            w_copy(d, 0, i).wait_send()
            d_copy(d, 1, i).wait_send()

            @pl.when((rd[d] != 3) | in_half(d, i))
            def _(d=d):
                w_copy(d, 1, i).wait_send()

            @pl.when((rd[d] != 0) | in_half(d, i))
            def _(d=d):
                d_copy(d, 0, i).wait_send()

        @pl.when(r == 0)
        def _():
            y_copy(0, i).wait_send()
            y_copy(1, i).wait_send()

        @pl.when(rd[1] == 1)
        def _():
            y2_copy(0, i).wait_send()

        @pl.when(rd[1] == 3)
        def _():
            y2_copy(1, i).wait_send()

        stored(i).wait()
        return 0

    lax.fori_loop(0, NC, leave, 0)
    for d in (0, 1):
        for k in (0, 1):
            g_copy(d, k).wait_send()
        g2_copy(d).wait_send()
    for n in (1, 2, 3):
        for copy in (s1_copy, s2_copy, s5_copy, s3_copy, xr_copy, q1_copy, q_copy, o_copy):
            copy(n).wait_send()

    for g in range(4):
        s4_copy(g).wait_send()
        ct_copy(g).wait_send()


def place(parts, shard, ig_out, wg_out, ig_held, wg_held, sem_in, sem_out):
    count, _, quarter = parts.shape
    rows = shard.shape[0] // count
    pairs = []
    for g in range(count):
        block = pl.ds(g * rows, rows)
        pairs.append((shard.at[block], wg_held.at[block], wg_out.at[block]))
    for g in range(count):
        columns = pl.ds(g * quarter, quarter)
        pairs.append((parts.at[g], ig_held.at[:, columns], ig_out.at[:, columns]))
    loads = [pltpu.make_async_copy(a, b, sem_in.at[n]) for n, (a, b, _) in enumerate(pairs)]
    stores = [pltpu.make_async_copy(b, c, sem_out.at[n]) for n, (_, b, c) in enumerate(pairs)]
    for load in loads:
        load.start()
    for load, store in zip(loads, stores, strict=True):
        load.wait()
        store.start()
    for store in stores:
        store.wait()


def per_device(inputs, out_grad, weight):
    tok, width = inputs.shape
    rows, hidden = weight.shape
    quarter = width // 4
    sems = pltpu.SemaphoreType.DMA
    hbm = pl.BlockSpec(memory_space=pl.ANY)
    parts, weight_grad = pl.pallas_call(
        kernel,
        out_shape=(
            jax.ShapeDtypeStruct((4, tok, quarter), BF16),
            jax.ShapeDtypeStruct((rows, hidden), BF16),
        ),
        in_specs=[hbm] * 3,
        out_specs=(hbm, hbm),
        scratch_shapes=[
            pltpu.VMEM((8 * tok, hidden), BF16),
            pltpu.VMEM((4, rows, hidden), BF16),
            pltpu.VMEM((4, 8 * tok, quarter), BF16),
            pltpu.VMEM((4, tok, quarter), BF16),
            pltpu.VMEM((4, tok, quarter), BF16),
            pltpu.VMEM((4, rows, hidden), F32),
            pltpu.VMEM((2, 3, rows, hidden), BF16),
            pltpu.VMEM((4, 8 * tok, quarter), BF16),
            pltpu.VMEM((4, 4 * tok, quarter), BF16),
            pltpu.VMEM((4, 4 * tok, quarter), BF16),
            pltpu.VMEM((4, 4 * tok, quarter), BF16),
            pltpu.VMEM((4 * tok, quarter), BF16),
            pltpu.VMEM((4, tok, quarter), BF16),
            pltpu.VMEM((4, tok, quarter), BF16),
            pltpu.VMEM((rows, hidden), BF16),
            sems((2, 2, NC)), sems((2, 2, NC)), sems((2, 2, NC)), sems((2, 2, NC)),
            sems((NC,)), sems((2, NC)), sems((2, NC)), sems((2, NC)), sems((NC,)),
            sems((2, 2)), sems((2, 2)), sems((2,)), sems((2,)),
            *[sems((4,)) for _ in range(20)],
            sems((4,)),
        ],
        compiler_params=pltpu.CompilerParams(
            collective_id=0, has_side_effects=True, vmem_limit_bytes=56 * 2**20
        ),
        cost_estimate=pl.CostEstimate(
            flops=4 * 8 * tok * width * hidden, bytes_accessed=4 * 2**20, transcendentals=0
        ),
        name="backward",
    )(inputs, out_grad, weight)
    return pl.pallas_call(
        place,
        out_shape=(
            jax.ShapeDtypeStruct((tok, width), BF16),
            jax.ShapeDtypeStruct((rows, hidden), BF16),
        ),
        in_specs=[hbm] * 2,
        out_specs=(hbm, hbm),
        scratch_shapes=[
            pltpu.VMEM((tok, width), BF16), pltpu.VMEM((rows, hidden), BF16), sems((8,)), sems((8,)),
        ],
        name="place",
    )(parts, weight_grad)


def solution(mesh):
    return jax.shard_map(
        per_device,
        mesh=mesh,
        in_specs=(P(("dp", "gx", "gz"), "gy"), P(("dp", "gx", "gy"), "gz"), P(("gy", "gx"), "gz")),
        out_specs=(P(("dp", "gx", "gz"), "gy"), P(("gy", "gx"), "gz")),
        check_vma=False,
    )
```

```python
import functools

import jax
import jax.numpy as jnp
from jax import lax
from jax.experimental import pallas as pl
from jax.experimental.pallas import tpu as pltpu
from jax.sharding import PartitionSpec as P

MESH = pl.DeviceIdType.MESH
NC = 8
UNIT = NC // 8
AHEAD = 1
LEAD = 2
HOP = 2
START = 12
BF16, F32 = jnp.bfloat16, jnp.float32


def kernel(
    inp, og, wt, O, wg_out,
    G, W, X, I1, I2, PT, RD, T, CT, S, XR, R, Q1, Q, FB,
    wr, ws, dr, dss, yr, ysd, y2r, y2s, kept, gr, gs, g2r, g2s, s1r, s1s, s2r, s2s, s3r, s3s, s4r, s4s, s5r, s5s,
    ctr, cts, xrr, xrs, qr, qs, q1r, q1s, orr, ors, loc,
):
    y, h, zl = lax.axis_index("dp"), lax.axis_index("gx"), lax.axis_index("gy")
    gz = lax.axis_index("gz")
    x, c = gz // 2, gz % 2
    z = h * 4 + zl
    r = (zl - y + 4) % 4
    tok = og.shape[0] // 2
    half = 4 * tok
    quarter = inp.shape[1] // 4
    rows = wt.shape[0] // NC

    def zdev(zz):
        return {"gx": zz // 4, "gy": zz % 4}

    def xdev(xx):
        return {"gz": xx * 2 + c}

    right = (zdev((z + 1) % 16), zdev((z + 15) % 16))
    ydev = ({"dp": (y + 1) % 4}, {"dp": (y + 3) % 4})
    core = {"gz": x * 2 + 1 - c}
    rd = (r, (4 - r) % 4)
    rr = tuple(jnp.where(v == 0, 4, v) for v in rd)
    sign = (1, -1)

    def held_from(d, cls):
        return ((z - sign[d] * (rd[d] + 4 * cls) + 32) % 16) // 4

    def bound_for(d, s):
        return ((z + sign[d] * (4 - rd[d] + 4 * (1 - s)) + 32) % 16) // 4

    def in_half(d, i):
        return i < NC // 2 if d == 0 else i >= NC // 2

    def remote(src, dst, send, recv, dev):
        return pltpu.make_async_remote_copy(
            src_ref=src, dst_ref=dst, send_sem=send, recv_sem=recv, device_id=dev, device_id_type=MESH
        )

    def tokens(first):
        return pl.ds(pl.multiple_of(first, 32), tok)

    def halves(which):
        return pl.ds(pl.multiple_of(which * half, 128), half)

    def chunk(i):
        return pl.ds(pl.multiple_of(i * rows, rows), rows)

    def chunk_half(i, d):
        return pl.ds(pl.multiple_of(i * rows + d * (rows // 2), rows // 2), rows // 2)

    def columns(q):
        return pl.ds(pl.multiple_of(q * quarter, 128), quarter)

    def w_copy(d, stream, i):
        part = W.at[held_from(d, stream), chunk(i)]
        return remote(part, part, ws.at[d, stream, i], wr.at[d, stream, i], right[d])

    def d_copy(d, s, i):
        to = s + jnp.where(rd[d] == 3, 1, 0)
        return remote(RD.at[d, s, chunk(i)], RD.at[d, to, chunk(i)], dss.at[d, s, i], dr.at[d, s, i], right[d])

    def y_copy(d, i):
        return remote(FB.at[chunk(i)], FB.at[chunk(i)], ysd.at[d, i], yr.at[i], ydev[d])

    def y2_copy(d, i):
        part = FB.at[chunk_half(i, d)]
        return remote(part, part, y2s.at[d, i], y2r.at[d, i], ydev[d])

    def stored(i):
        return pltpu.make_async_copy(FB.at[chunk(i)], wg_out.at[chunk(i)], kept.at[i])

    def g_copy(d, k):
        part = G.at[tokens(k * half + y * tok)]
        return remote(part, part, gs.at[d, k], gr.at[d, k], ydev[d])

    def g2_copy(d):
        part = G.at[tokens(d * half + ((y + 3 + 2 * d) % 4) * tok)]
        return remote(part, part, g2s.at[d], g2r.at[d], ydev[d])

    def s1_copy(dx):
        to = (x + dx) % 4
        return remote(inp.at[:, columns(to)], I1.at[x], s1s.at[dx], s1r.at[x], xdev(to))

    def s2_copy(t):
        to = (zl + t) % 4
        return remote(I1.at[to], I2.at[zl], s2s.at[t], s2r.at[zl], {"gy": to})

    def s5_copy(t):
        to = (y + t) % 4
        return remote(I2.at[to], X.at[x, tokens(c * half + y * tok)], s5s.at[t], s5r.at[y], {"dp": to})

    def s3_copy(dx):
        part = X.at[x, halves(c)]
        return remote(part, part, s3s.at[dx], s3r.at[x], xdev((x + dx) % 4))

    def s4_copy(g):
        part = X.at[g, halves(c)]
        return remote(part, part, s4s.at[g], s4r.at[g], core)

    def ct_copy(g):
        return remote(T.at[g, halves(1 - c)], CT.at[g], cts.at[g], ctr.at[g], core)

    def xr_copy(dx):
        to = (x + dx) % 4
        return remote(S.at[to], XR.at[x], xrs.at[dx], xrr.at[x], xdev(to))

    def q1_copy(t):
        to = (y + t) % 4
        return remote(R.at[tokens(to * tok)], Q1.at[y], q1s.at[t], q1r.at[y], {"dp": to})

    def q_copy(t):
        to = (zl + t) % 4
        return remote(Q1.at[to], Q.at[zl], qs.at[t], qr.at[zl], {"gy": to})

    def o_copy(dx):
        to = (x + dx) % 4
        return remote(Q.at[to], O.at[x], ors.at[dx], orr.at[x], xdev(to))

    def arrived(dst, send, recv, dev):
        remote(dst, dst, send, recv, dev).wait_recv()

    barrier = pltpu.get_barrier_semaphore()

    def greet(dev):
        pl.semaphore_signal(barrier, inc=1, device_id=dev, device_id_type=MESH)

    for dev in (*right, core):
        greet(dev)
    for t in (1, 2, 3):
        greet(xdev((x + t) % 4))
        greet({"dp": (y + t) % 4})
        greet({"gy": (zl + t) % 4})
    own = [
        pltpu.make_async_copy(og.at[pl.ds(k * tok, tok)], G.at[tokens(k * half + y * tok)], loc.at[k]) for k in (0, 1)
    ]
    own.append(pltpu.make_async_copy(inp.at[:, columns(x)], I1.at[x], loc.at[2]))
    for copy in own:
        copy.start()

    @pl.when(r == 0)
    def _():
        held = pltpu.make_async_copy(wt, W.at[h], loc.at[3])
        held.start()
        held.wait()

    pl.semaphore_wait(barrier, 12)
    for dx in (1, 2, 3):
        s1_copy(dx).start()
    for copy in own:
        copy.wait()
    for d in (0, 1):
        g_copy(d, d).start()

    def w_own(i):
        @pl.when((r == 0) & (i < NC))
        def _():
            w_copy(0, 0, i).start()
            w_copy(1, 0, i).start()

    for i in range(AHEAD):
        w_own(i)

    def w_step(d, s):
        m = s - HOP * rr[d]

        @pl.when((m >= 0) & (m < 2 * NC))
        def _():
            stream, i = m // NC, m % NC
            cls = stream + jnp.where(rd[d] == 0, 1, 0)

            @pl.when((cls < 2) | in_half(d, i))
            def _():
                part = W.at[held_from(d, cls), chunk(i)]
                arrived(part, ws.at[d, 0, 0], wr.at[d, stream, i], right[d])

            @pl.when((cls == 0) | ((cls == 1) & ((rd[d] != 3) | in_half(d, i))))
            def _():
                w_copy(d, cls, i).start()

    def add(d, s, i, received):
        own_term = PT[bound_for(d, s), chunk(i), :]
        if received:
            own_term = own_term + RD[d, s, chunk(i), :].astype(F32)
        RD[d, s, chunk(i), :] = own_term.astype(BF16)
        d_copy(d, s, i).start()

    def d_step(d, s):
        @pl.when((rd[d] == 0) & (s >= 0) & (s < NC))
        def _():
            @pl.when(in_half(d, s))
            def _():
                add(d, 0, s, False)

        m = s - HOP * rr[d]

        @pl.when((m >= 0) & (m < 2 * NC))
        def _():
            stream, i = m // NC, m % NC
            slot = stream + jnp.where(rd[d] == 0, 1, 0)
            expected = (slot > 0) | (rd[d] > 1) | in_half(d, i)

            @pl.when(expected)
            def _():
                arrived(RD.at[d, slot, chunk(i)], dss.at[d, 0, 0], dr.at[d, stream, i], right[d])

            @pl.when((slot < 2) & expected)
            def _():
                add(d, slot, i, True)

            @pl.when((slot < 2) & jnp.logical_not(expected))
            def _():
                add(d, slot, i, False)

    groups = 4

    def last_step(s):
        i = s - HOP * 4 - NC

        @pl.when((r == 0) & (i >= 0) & (i < NC))
        def _():
            total = PT[h, chunk(i), :] + RD[0, 2, chunk(i), :].astype(F32) + RD[1, 2, chunk(i), :].astype(F32)
            mean = (total / groups).astype(BF16)
            FB[chunk(i), :] = mean
            y_copy(0, i).start()
            y_copy(1, i).start()
            stored(i).start()

        away = rd[1]
        n = i - HOP * jnp.where(away == 2, 2, 1)

        @pl.when((r != 0) & (n >= 0) & (n < NC))
        def _():
            @pl.when(away != 2)
            def _():
                arrived(FB.at[chunk(n)], ysd.at[0, 0], yr.at[n], ydev[0])

            @pl.when(away == 1)
            def _():
                y2_copy(0, n).start()

            @pl.when(away == 3)
            def _():
                y2_copy(1, n).start()

            @pl.when(away == 2)
            def _():
                for d in (0, 1):
                    arrived(FB.at[chunk_half(n, d)], y2s.at[0, 0], y2r.at[d, n], ydev[0])

            stored(n).start()

    def in_places():
        for dx in (1, 2, 3):
            j = (x + dx) % 4
            arrived(I1.at[j], s1s.at[0], s1r.at[j], core)

        for t in (1, 2, 3):
            s2_copy(t).start()
        I2[zl] = I1[zl]

    def in_columns():
        for t in (1, 2, 3):
            j = (zl + t) % 4
            arrived(I2.at[j], s2s.at[0], s2r.at[j], core)
        for t in (1, 2, 3):
            s5_copy(t).start()
        for d in (0, 1):
            g_copy(d, 1 - d).start()
        X[x, tokens(c * half + y * tok), :] = I2[y]

    def grad_relay():
        for d in (0, 1):
            k = (y + 3 + 2 * d) % 4
            arrived(G.at[tokens(d * half + k * tok)], gs.at[0, 0], gr.at[d, d], core)
            g2_copy(d).start()

    def in_spread():
        for t in (1, 2, 3):
            k = (y + t) % 4
            arrived(X.at[x, tokens(c * half + k * tok)], s5s.at[0], s5r.at[k], core)
        for dx in (1, 2, 3):
            s3_copy(dx).start()
        s4_copy(x).start()

    def in_cores():
        for dx in (1, 2, 3):
            g = (x + dx) % 4
            arrived(X.at[g, halves(c)], s3s.at[0], s3r.at[g], core)
            s4_copy(g).start()

    def in_done():
        for g in range(4):
            arrived(X.at[g, halves(1 - c)], s4s.at[0], s4r.at[g], core)
        for d in (0, 1):
            k = (y + 3 + 2 * d) % 4
            arrived(G.at[tokens((1 - d) * half + k * tok)], gs.at[0, 0], gr.at[d, 1 - d], core)
            k = (y + 2) % 4
            arrived(G.at[tokens(d * half + k * tok)], g2s.at[0], g2r.at[d], core)

    def p_job(g):
        def tile(n, _):
            cols = pl.ds(pl.multiple_of(n * 256, 256), 256)
            PT[g, :, cols] = lax.dot_general(
                X[g], G[:, cols], (((0,), (0,)), ((), ())), preferred_element_type=F32
            )
            return 0

        lax.fori_loop(0, G.shape[1] // 256, tile, 0)

    def t_job(g, n):
        where = halves((1 - c + n) % 2)
        T[g, where, :] = lax.dot_general(
            G[where, :], W[g], (((1,), (1,)), ((), ())), preferred_element_type=F32
        ).astype(BF16)

        @pl.when(n == 0)
        def _():
            ct_copy(g).start()

    def cores_sum(g):
        arrived(CT.at[g], cts.at[0], ctr.at[g], core)
        S[g] = (T[g, halves(c), :].astype(F32) + CT[g].astype(F32)).astype(BF16)

    def x_send():
        for g in range(4):
            cores_sum(g)
        for dx in (1, 2, 3):
            xr_copy(dx).start()

    def x_sum():
        total = S[x].astype(F32)
        for dx in (1, 2, 3):
            g = (x + dx) % 4
            arrived(XR.at[g], xrs.at[0], xrr.at[g], core)
            total = total + XR[g].astype(F32)
        R[...] = total.astype(BF16)

        for t in (1, 2, 3):
            q1_copy(t).start()
        Q1[y] = R[tokens(y * tok), :]

    def out_planes():
        for t in (1, 2, 3):
            f = (y + t) % 4
            arrived(Q1.at[f], q1s.at[0], q1r.at[f], core)
        for t in (1, 2, 3):
            q_copy(t).start()
        Q[zl] = Q1[zl]

    def out_spread():
        for t in (1, 2, 3):
            j = (zl + t) % 4
            arrived(Q.at[j], qs.at[0], qr.at[j], core)
        for dx in (1, 2, 3):
            o_copy(dx).start()
        pltpu.make_async_copy(Q.at[x], O.at[x], loc.at[0]).start()

    def out_done():
        for dx in (1, 2, 3):
            g = (x + dx) % 4
            arrived(O.at[g], ors.at[0], orr.at[g], core)
        pltpu.make_async_copy(Q.at[x], O.at[x], loc.at[0]).wait()

    p_jobs = (
        bound_for(0, 0),
        jnp.where(r == 0, h, bound_for(1, 0)),
        bound_for(0, 1),
        bound_for(1, 1),
    )
    t_jobs = (
        held_from(0, 0),
        jnp.where(r == 0, held_from(0, 1), held_from(1, 0)),
        jnp.where(r == 0, held_from(1, 1), held_from(0, 1)),
        jnp.where(r == 0, held_from(0, 2), held_from(1, 1)),
    )
    late = 2 * NC + 4 * HOP

    def pick(s, pairs, jobs):
        g = jobs[0]
        for at, job in zip(pairs[1:], jobs[1:], strict=True):
            g = jnp.where(s == at, job, g)
        return g

    p_at = (START, START + 1, START + 2 + UNIT, START + 2 + 2 * UNIT)
    t_at = (*(START + 3 * UNIT + k for k in range(4)), *(late - 1 + k for k in range(4)))

    def step(s, _):
        w_own(s + AHEAD)
        for d in (0, 1):
            w_step(d, s)
        for at, job in (
            (0, in_places), (2 * UNIT, in_columns), (4 * UNIT, grad_relay),
            (5 * UNIT, in_spread), (8 * UNIT, in_cores), (START, in_done),
        ):
            pl.when(s == at)(job)

        @pl.when(functools.reduce(jnp.logical_or, [s == at for at in p_at]))
        def _():
            p_job(pick(s, p_at, p_jobs))

        for d in (0, 1):
            d_step(d, s - START - LEAD)
        last_step(s - START - LEAD)

        @pl.when(functools.reduce(jnp.logical_or, [s == at for at in t_at]))
        def _():
            n = functools.reduce(jnp.logical_or, [s == at for at in t_at[1::2]]).astype(jnp.int32)
            t_job(pick(s, t_at, [g for g in t_jobs for _ in (0, 1)]), n)

        for at, job in (
            (late + 3, x_send), (late + 3 + 4 * UNIT, x_sum), (late + 3 + 7 * UNIT, out_planes),
            (late + 3 + 10 * UNIT, out_spread),
        ):
            pl.when(s == at)(job)
        return 0

    lax.fori_loop(0, START + LEAD + 2 * NC + 6 * HOP, step, 0)
    out_done()

    def leave(i, _):
        for d in (0, 1):
            w_copy(d, 0, i).wait_send()
            d_copy(d, 1, i).wait_send()

            @pl.when((rd[d] != 3) | in_half(d, i))
            def _(d=d):
                w_copy(d, 1, i).wait_send()

            @pl.when((rd[d] != 0) | in_half(d, i))
            def _(d=d):
                d_copy(d, 0, i).wait_send()

        @pl.when(r == 0)
        def _():
            y_copy(0, i).wait_send()
            y_copy(1, i).wait_send()

        @pl.when(rd[1] == 1)
        def _():
            y2_copy(0, i).wait_send()

        @pl.when(rd[1] == 3)
        def _():
            y2_copy(1, i).wait_send()

        stored(i).wait()
        return 0

    lax.fori_loop(0, NC, leave, 0)
    for d in (0, 1):
        for k in (0, 1):
            g_copy(d, k).wait_send()
        g2_copy(d).wait_send()
    for n in (1, 2, 3):
        for copy in (s1_copy, s2_copy, s5_copy, s3_copy, xr_copy, q1_copy, q_copy, o_copy):
            copy(n).wait_send()

    for g in range(4):
        s4_copy(g).wait_send()
        ct_copy(g).wait_send()


def place(parts, shard, ig_out, wg_out, ig_held, wg_held, sem_in, sem_out):
    count, _, quarter = parts.shape
    rows = shard.shape[0] // count
    pairs = []
    for g in range(count):
        block = pl.ds(g * rows, rows)
        pairs.append((shard.at[block], wg_held.at[block], wg_out.at[block]))
    for g in range(count):
        columns = pl.ds(g * quarter, quarter)
        pairs.append((parts.at[g], ig_held.at[:, columns], ig_out.at[:, columns]))
    loads = [pltpu.make_async_copy(a, b, sem_in.at[n]) for n, (a, b, _) in enumerate(pairs)]
    stores = [pltpu.make_async_copy(b, c, sem_out.at[n]) for n, (_, b, c) in enumerate(pairs)]
    for load in loads:
        load.start()
    for load, store in zip(loads, stores, strict=True):
        load.wait()
        store.start()
    for store in stores:
        store.wait()


def per_device(inputs, out_grad, weight):
    tok, width = inputs.shape
    rows, hidden = weight.shape
    quarter = width // 4
    sems = pltpu.SemaphoreType.DMA
    hbm = pl.BlockSpec(memory_space=pl.ANY)
    parts, weight_grad = pl.pallas_call(
        kernel,
        out_shape=(
            jax.ShapeDtypeStruct((4, tok, quarter), BF16),
            jax.ShapeDtypeStruct((rows, hidden), BF16),
        ),
        in_specs=[hbm] * 3,
        out_specs=(hbm, hbm),
        scratch_shapes=[
            pltpu.VMEM((8 * tok, hidden), BF16),
            pltpu.VMEM((4, rows, hidden), BF16),
            pltpu.VMEM((4, 8 * tok, quarter), BF16),
            pltpu.VMEM((4, tok, quarter), BF16),
            pltpu.VMEM((4, tok, quarter), BF16),
            pltpu.VMEM((4, rows, hidden), F32),
            pltpu.VMEM((2, 3, rows, hidden), BF16),
            pltpu.VMEM((4, 8 * tok, quarter), BF16),
            pltpu.VMEM((4, 4 * tok, quarter), BF16),
            pltpu.VMEM((4, 4 * tok, quarter), BF16),
            pltpu.VMEM((4, 4 * tok, quarter), BF16),
            pltpu.VMEM((4 * tok, quarter), BF16),
            pltpu.VMEM((4, tok, quarter), BF16),
            pltpu.VMEM((4, tok, quarter), BF16),
            pltpu.VMEM((rows, hidden), BF16),
            sems((2, 2, NC)), sems((2, 2, NC)), sems((2, 2, NC)), sems((2, 2, NC)),
            sems((NC,)), sems((2, NC)), sems((2, NC)), sems((2, NC)), sems((NC,)),
            sems((2, 2)), sems((2, 2)), sems((2,)), sems((2,)),
            *[sems((4,)) for _ in range(20)],
            sems((4,)),
        ],
        compiler_params=pltpu.CompilerParams(
            collective_id=0, has_side_effects=True, vmem_limit_bytes=56 * 2**20
        ),
        cost_estimate=pl.CostEstimate(
            flops=4 * 8 * tok * width * hidden, bytes_accessed=4 * 2**20, transcendentals=0
        ),
        name="backward",
    )(inputs, out_grad, weight)
    return pl.pallas_call(
        place,
        out_shape=(
            jax.ShapeDtypeStruct((tok, width), BF16),
            jax.ShapeDtypeStruct((rows, hidden), BF16),
        ),
        in_specs=[hbm] * 2,
        out_specs=(hbm, hbm),
        scratch_shapes=[
            pltpu.VMEM((tok, width), BF16), pltpu.VMEM((rows, hidden), BF16), sems((8,)), sems((8,)),
        ],
        name="place",
    )(parts, weight_grad)


def solution(mesh):
    return jax.shard_map(
        per_device,
        mesh=mesh,
        in_specs=(P(("dp", "gx", "gz"), "gy"), P(("dp", "gx", "gy"), "gz"), P(("gy", "gx"), "gz")),
        out_specs=(P(("dp", "gx", "gz"), "gy"), P(("gy", "gx"), "gz")),
        check_vma=False,
    )
```

```python
import functools

import jax
import jax.numpy as jnp
from jax import lax
from jax.experimental import pallas as pl
from jax.experimental.pallas import tpu as pltpu
from jax.sharding import PartitionSpec as P

MESH = pl.DeviceIdType.MESH
NC = 8
UNIT = NC // 8
AHEAD = 1
LEAD = 2
HOP = 2
START = 12
BF16, F32 = jnp.bfloat16, jnp.float32


def kernel(
    inp, og, wt, O, wg_out,
    G, W, X, I1, I2, PT, RD, T, CT, S, XR, R, Q1, Q, FB,
    wr, ws, dr, dss, yr, ysd, y2r, y2s, kept, gr, gs, g2r, g2s, s1r, s1s, s2r, s2s, s3r, s3s, s4r, s4s, s5r, s5s,
    ctr, cts, xrr, xrs, qr, qs, q1r, q1s, orr, ors, loc,
):
    y, h, zl = lax.axis_index("dp"), lax.axis_index("gx"), lax.axis_index("gy")
    gz = lax.axis_index("gz")
    x, c = gz // 2, gz % 2
    z = h * 4 + zl
    r = (zl - y + 4) % 4
    tok = og.shape[0] // 2
    half = 4 * tok
    quarter = inp.shape[1] // 4
    rows = wt.shape[0] // NC

    def zdev(zz):
        return {"gx": zz // 4, "gy": zz % 4}

    def xdev(xx):
        return {"gz": xx * 2 + c}

    right = (zdev((z + 1) % 16), zdev((z + 15) % 16))
    ydev = ({"dp": (y + 1) % 4}, {"dp": (y + 3) % 4})
    core = {"gz": x * 2 + 1 - c}
    rd = (r, (4 - r) % 4)
    rr = tuple(jnp.where(v == 0, 4, v) for v in rd)
    sign = (1, -1)

    def held_from(d, cls):
        return ((z - sign[d] * (rd[d] + 4 * cls) + 32) % 16) // 4

    def bound_for(d, s):
        return ((z + sign[d] * (4 - rd[d] + 4 * (1 - s)) + 32) % 16) // 4

    def in_half(d, i):
        return i < NC // 2 if d == 0 else i >= NC // 2

    def remote(src, dst, send, recv, dev):
        return pltpu.make_async_remote_copy(
            src_ref=src, dst_ref=dst, send_sem=send, recv_sem=recv, device_id=dev, device_id_type=MESH
        )

    def tokens(first):
        return pl.ds(pl.multiple_of(first, 32), tok)

    def halves(which):
        return pl.ds(pl.multiple_of(which * half, 128), half)

    def chunk(i):
        return pl.ds(pl.multiple_of(i * rows, rows), rows)

    def chunk_half(i, d):
        return pl.ds(pl.multiple_of(i * rows + d * (rows // 2), rows // 2), rows // 2)

    def columns(q):
        return pl.ds(pl.multiple_of(q * quarter, 128), quarter)

    def w_copy(d, stream, i):
        part = W.at[held_from(d, stream), chunk(i)]
        return remote(part, part, ws.at[d, stream, i], wr.at[d, stream, i], right[d])

    def d_copy(d, s, i):
        to = s + jnp.where(rd[d] == 3, 1, 0)
        return remote(RD.at[d, s, chunk(i)], RD.at[d, to, chunk(i)], dss.at[d, s, i], dr.at[d, s, i], right[d])

    def y_copy(d, i):
        return remote(FB.at[chunk(i)], FB.at[chunk(i)], ysd.at[d, i], yr.at[i], ydev[d])

    def y2_copy(d, i):
        part = FB.at[chunk_half(i, d)]
        return remote(part, part, y2s.at[d, i], y2r.at[d, i], ydev[d])

    def stored(i):
        return pltpu.make_async_copy(FB.at[chunk(i)], wg_out.at[chunk(i)], kept.at[i])

    def g_copy(d, k):
        part = G.at[tokens(k * half + y * tok)]
        return remote(part, part, gs.at[d, k], gr.at[d, k], ydev[d])

    def g2_copy(d):
        part = G.at[tokens(d * half + ((y + 3 + 2 * d) % 4) * tok)]
        return remote(part, part, g2s.at[d], g2r.at[d], ydev[d])

    def s1_copy(dx):
        to = (x + dx) % 4
        return remote(inp.at[:, columns(to)], I1.at[x], s1s.at[dx], s1r.at[x], xdev(to))

    def s2_copy(t):
        to = (zl + t) % 4
        return remote(I1.at[to], I2.at[zl], s2s.at[t], s2r.at[zl], {"gy": to})

    def s5_copy(t):
        to = (y + t) % 4
        return remote(I2.at[to], X.at[x, tokens(c * half + y * tok)], s5s.at[t], s5r.at[y], {"dp": to})

    def s3_copy(dx):
        part = X.at[x, halves(c)]
        return remote(part, part, s3s.at[dx], s3r.at[x], xdev((x + dx) % 4))

    def s4_copy(g):
        part = X.at[g, halves(c)]
        return remote(part, part, s4s.at[g], s4r.at[g], core)

    def ct_copy(g):
        return remote(T.at[g, halves(1 - c)], CT.at[g], cts.at[g], ctr.at[g], core)

    def xr_copy(dx):
        to = (x + dx) % 4
        return remote(S.at[to], XR.at[x], xrs.at[dx], xrr.at[x], xdev(to))

    def q1_copy(t):
        to = (y + t) % 4
        return remote(R.at[tokens(to * tok)], Q1.at[y], q1s.at[t], q1r.at[y], {"dp": to})

    def q_copy(t):
        to = (zl + t) % 4
        return remote(Q1.at[to], Q.at[zl], qs.at[t], qr.at[zl], {"gy": to})

    def o_copy(dx):
        to = (x + dx) % 4
        return remote(Q.at[to], O.at[x], ors.at[dx], orr.at[x], xdev(to))

    def arrived(dst, send, recv, dev):
        remote(dst, dst, send, recv, dev).wait_recv()

    barrier = pltpu.get_barrier_semaphore()

    def greet(dev):
        pl.semaphore_signal(barrier, inc=1, device_id=dev, device_id_type=MESH)

    for dev in (*right, core):
        greet(dev)
    for t in (1, 2, 3):
        greet(xdev((x + t) % 4))
        greet({"dp": (y + t) % 4})
        greet({"gy": (zl + t) % 4})
    own = [
        pltpu.make_async_copy(og.at[pl.ds(k * tok, tok)], G.at[tokens(k * half + y * tok)], loc.at[k]) for k in (0, 1)
    ]
    own.append(pltpu.make_async_copy(inp.at[:, columns(x)], I1.at[x], loc.at[2]))
    for copy in own:
        copy.start()

    @pl.when(r == 0)
    def _():
        held = pltpu.make_async_copy(wt, W.at[h], loc.at[3])
        held.start()
        held.wait()

    pl.semaphore_wait(barrier, 12)
    for dx in (1, 2, 3):
        s1_copy(dx).start()
    for copy in own:
        copy.wait()
    for d in (0, 1):
        g_copy(d, d).start()

    def w_own(i):
        @pl.when((r == 0) & (i < NC))
        def _():
            w_copy(0, 0, i).start()
            w_copy(1, 0, i).start()

    for i in range(AHEAD):
        w_own(i)

    def w_step(d, s):
        m = s - HOP * rr[d]

        @pl.when((m >= 0) & (m < 2 * NC))
        def _():
            stream, i = m // NC, m % NC
            cls = stream + jnp.where(rd[d] == 0, 1, 0)

            @pl.when((cls < 2) | in_half(d, i))
            def _():
                part = W.at[held_from(d, cls), chunk(i)]
                arrived(part, ws.at[d, 0, 0], wr.at[d, stream, i], right[d])

            @pl.when((cls == 0) | ((cls == 1) & ((rd[d] != 3) | in_half(d, i))))
            def _():
                w_copy(d, cls, i).start()

    def add(d, s, i, received):
        own_term = PT[bound_for(d, s), chunk(i), :]
        if received:
            own_term = own_term + RD[d, s, chunk(i), :].astype(F32)
        RD[d, s, chunk(i), :] = own_term.astype(BF16)
        d_copy(d, s, i).start()

    def d_step(d, s):
        @pl.when((rd[d] == 0) & (s >= 0) & (s < NC))
        def _():
            @pl.when(in_half(d, s))
            def _():
                add(d, 0, s, False)

        m = s - HOP * rr[d]

        @pl.when((m >= 0) & (m < 2 * NC))
        def _():
            stream, i = m // NC, m % NC
            slot = stream + jnp.where(rd[d] == 0, 1, 0)
            expected = (slot > 0) | (rd[d] > 1) | in_half(d, i)

            @pl.when(expected)
            def _():
                arrived(RD.at[d, slot, chunk(i)], dss.at[d, 0, 0], dr.at[d, stream, i], right[d])

            @pl.when((slot < 2) & expected)
            def _():
                add(d, slot, i, True)

            @pl.when((slot < 2) & jnp.logical_not(expected))
            def _():
                add(d, slot, i, False)

    groups = 4

    def last_step(s):
        i = s - HOP * 4 - NC

        @pl.when((r == 0) & (i >= 0) & (i < NC))
        def _():
            total = PT[h, chunk(i), :] + RD[0, 2, chunk(i), :].astype(F32) + RD[1, 2, chunk(i), :].astype(F32)
            mean = (total / groups).astype(BF16)
            FB[chunk(i), :] = mean
            y_copy(0, i).start()
            y_copy(1, i).start()
            stored(i).start()

        away = rd[1]
        n = i - HOP * jnp.where(away == 2, 2, 1)

        @pl.when((r != 0) & (n >= 0) & (n < NC))
        def _():
            @pl.when(away != 2)
            def _():
                arrived(FB.at[chunk(n)], ysd.at[0, 0], yr.at[n], ydev[0])

            @pl.when(away == 1)
            def _():
                y2_copy(0, n).start()

            @pl.when(away == 3)
            def _():
                y2_copy(1, n).start()

            @pl.when(away == 2)
            def _():
                for d in (0, 1):
                    arrived(FB.at[chunk_half(n, d)], y2s.at[0, 0], y2r.at[d, n], ydev[0])

            stored(n).start()

    def in_places():
        for dx in (1, 2, 3):
            j = (x + dx) % 4
            arrived(I1.at[j], s1s.at[0], s1r.at[j], core)

        for t in (1, 2, 3):
            s2_copy(t).start()
        I2[zl] = I1[zl]

    def in_columns():
        for t in (1, 2, 3):
            j = (zl + t) % 4
            arrived(I2.at[j], s2s.at[0], s2r.at[j], core)
        for t in (1, 2, 3):
            s5_copy(t).start()
        for d in (0, 1):
            g_copy(d, 1 - d).start()
        X[x, tokens(c * half + y * tok), :] = I2[y]

    def grad_relay():
        for d in (0, 1):
            k = (y + 3 + 2 * d) % 4
            arrived(G.at[tokens(d * half + k * tok)], gs.at[0, 0], gr.at[d, d], core)
            g2_copy(d).start()

    def in_spread():
        for t in (1, 2, 3):
            k = (y + t) % 4
            arrived(X.at[x, tokens(c * half + k * tok)], s5s.at[0], s5r.at[k], core)
        for dx in (1, 2, 3):
            s3_copy(dx).start()
        s4_copy(x).start()

    def in_cores():
        for dx in (1, 2, 3):
            g = (x + dx) % 4
            arrived(X.at[g, halves(c)], s3s.at[0], s3r.at[g], core)
            s4_copy(g).start()

    def in_done():
        for g in range(4):
            arrived(X.at[g, halves(1 - c)], s4s.at[0], s4r.at[g], core)
        for d in (0, 1):
            k = (y + 3 + 2 * d) % 4
            arrived(G.at[tokens((1 - d) * half + k * tok)], gs.at[0, 0], gr.at[d, 1 - d], core)
            k = (y + 2) % 4
            arrived(G.at[tokens(d * half + k * tok)], g2s.at[0], g2r.at[d], core)

    def p_job(g):
        def tile(n, _):
            cols = pl.ds(pl.multiple_of(n * 256, 256), 256)
            PT[g, :, cols] = lax.dot_general(
                X[g], G[:, cols], (((0,), (0,)), ((), ())), preferred_element_type=F32
            )
            return 0

        lax.fori_loop(0, G.shape[1] // 256, tile, 0)

    def t_job(g, n):
        where = halves((1 - c + n) % 2)
        T[g, where, :] = lax.dot_general(
            G[where, :], W[g], (((1,), (1,)), ((), ())), preferred_element_type=F32
        ).astype(BF16)

        @pl.when(n == 0)
        def _():
            ct_copy(g).start()

    def cores_sum(g):
        arrived(CT.at[g], cts.at[0], ctr.at[g], core)
        S[g] = (T[g, halves(c), :].astype(F32) + CT[g].astype(F32)).astype(BF16)

    def x_send(g):
        cores_sum(g)

        @pl.when(g != x)
        def _():
            xr_copy((g - x + 4) % 4).start()

    def x_sum():
        total = S[x].astype(F32)
        for dx in (1, 2, 3):
            g = (x + dx) % 4
            arrived(XR.at[g], xrs.at[0], xrr.at[g], core)
            total = total + XR[g].astype(F32)
        R[...] = total.astype(BF16)

        for t in (1, 2, 3):
            q1_copy(t).start()
        Q1[y] = R[tokens(y * tok), :]

    def out_planes():
        for t in (1, 2, 3):
            f = (y + t) % 4
            arrived(Q1.at[f], q1s.at[0], q1r.at[f], core)
        for t in (1, 2, 3):
            q_copy(t).start()
        Q[zl] = Q1[zl]

    def out_spread():
        for t in (1, 2, 3):
            j = (zl + t) % 4
            arrived(Q.at[j], qs.at[0], qr.at[j], core)
        for dx in (1, 2, 3):
            o_copy(dx).start()
        pltpu.make_async_copy(Q.at[x], O.at[x], loc.at[0]).start()

    def out_done():
        for dx in (1, 2, 3):
            g = (x + dx) % 4
            arrived(O.at[g], ors.at[0], orr.at[g], core)
        pltpu.make_async_copy(Q.at[x], O.at[x], loc.at[0]).wait()

    p_jobs = (
        bound_for(0, 0),
        jnp.where(r == 0, h, bound_for(1, 0)),
        bound_for(0, 1),
        bound_for(1, 1),
    )
    t_jobs = (
        held_from(0, 0),
        jnp.where(r == 0, held_from(0, 1), held_from(1, 0)),
        jnp.where(r == 0, held_from(1, 1), held_from(0, 1)),
        jnp.where(r == 0, held_from(0, 2), held_from(1, 1)),
    )
    late = 2 * NC + 4 * HOP

    def pick(s, pairs, jobs):
        g = jobs[0]
        for at, job in zip(pairs[1:], jobs[1:], strict=True):
            g = jnp.where(s == at, job, g)
        return g

    p_at = (START, START + 1, START + 2 + UNIT, START + 2 + 2 * UNIT)
    t_at = (*(START + 3 * UNIT + k for k in range(4)), *(late - 1 + k for k in range(4)))
    x_at = (START + 8 * UNIT, START + 9 * UNIT, late + 2, late + 4)

    def step(s, _):
        w_own(s + AHEAD)
        for d in (0, 1):
            w_step(d, s)
        for at, job in (
            (0, in_places), (2 * UNIT, in_columns), (4 * UNIT, grad_relay),
            (5 * UNIT, in_spread), (8 * UNIT, in_cores), (START, in_done),
        ):
            pl.when(s == at)(job)

        @pl.when(functools.reduce(jnp.logical_or, [s == at for at in p_at]))
        def _():
            p_job(pick(s, p_at, p_jobs))

        for d in (0, 1):
            d_step(d, s - START - LEAD)
        last_step(s - START - LEAD)

        @pl.when(functools.reduce(jnp.logical_or, [s == at for at in t_at]))
        def _():
            n = functools.reduce(jnp.logical_or, [s == at for at in t_at[1::2]]).astype(jnp.int32)
            t_job(pick(s, t_at, [g for g in t_jobs for _ in (0, 1)]), n)

        @pl.when(functools.reduce(jnp.logical_or, [s == at for at in x_at]))
        def _():
            x_send(pick(s, x_at, t_jobs))

        for at, job in (
            (late + 3 + 4 * UNIT, x_sum), (late + 3 + 7 * UNIT, out_planes),
            (late + 3 + 10 * UNIT, out_spread),
        ):
            pl.when(s == at)(job)
        return 0

    lax.fori_loop(0, START + LEAD + 2 * NC + 6 * HOP, step, 0)
    out_done()

    def leave(i, _):
        for d in (0, 1):
            w_copy(d, 0, i).wait_send()
            d_copy(d, 1, i).wait_send()

            @pl.when((rd[d] != 3) | in_half(d, i))
            def _(d=d):
                w_copy(d, 1, i).wait_send()

            @pl.when((rd[d] != 0) | in_half(d, i))
            def _(d=d):
                d_copy(d, 0, i).wait_send()

        @pl.when(r == 0)
        def _():
            y_copy(0, i).wait_send()
            y_copy(1, i).wait_send()

        @pl.when(rd[1] == 1)
        def _():
            y2_copy(0, i).wait_send()

        @pl.when(rd[1] == 3)
        def _():
            y2_copy(1, i).wait_send()

        stored(i).wait()
        return 0

    lax.fori_loop(0, NC, leave, 0)
    for d in (0, 1):
        for k in (0, 1):
            g_copy(d, k).wait_send()
        g2_copy(d).wait_send()
    for n in (1, 2, 3):
        for copy in (s1_copy, s2_copy, s5_copy, s3_copy, xr_copy, q1_copy, q_copy, o_copy):
            copy(n).wait_send()

    for g in range(4):
        s4_copy(g).wait_send()
        ct_copy(g).wait_send()


def place(parts, shard, ig_out, wg_out, ig_held, wg_held, sem_in, sem_out):
    count, _, quarter = parts.shape
    rows = shard.shape[0] // count
    pairs = []
    for g in range(count):
        block = pl.ds(g * rows, rows)
        pairs.append((shard.at[block], wg_held.at[block], wg_out.at[block]))
    for g in range(count):
        columns = pl.ds(g * quarter, quarter)
        pairs.append((parts.at[g], ig_held.at[:, columns], ig_out.at[:, columns]))
    loads = [pltpu.make_async_copy(a, b, sem_in.at[n]) for n, (a, b, _) in enumerate(pairs)]
    stores = [pltpu.make_async_copy(b, c, sem_out.at[n]) for n, (_, b, c) in enumerate(pairs)]
    for load in loads:
        load.start()
    for load, store in zip(loads, stores, strict=True):
        load.wait()
        store.start()
    for store in stores:
        store.wait()


def per_device(inputs, out_grad, weight):
    tok, width = inputs.shape
    rows, hidden = weight.shape
    quarter = width // 4
    sems = pltpu.SemaphoreType.DMA
    hbm = pl.BlockSpec(memory_space=pl.ANY)
    parts, weight_grad = pl.pallas_call(
        kernel,
        out_shape=(
            jax.ShapeDtypeStruct((4, tok, quarter), BF16),
            jax.ShapeDtypeStruct((rows, hidden), BF16),
        ),
        in_specs=[hbm] * 3,
        out_specs=(hbm, hbm),
        scratch_shapes=[
            pltpu.VMEM((8 * tok, hidden), BF16),
            pltpu.VMEM((4, rows, hidden), BF16),
            pltpu.VMEM((4, 8 * tok, quarter), BF16),
            pltpu.VMEM((4, tok, quarter), BF16),
            pltpu.VMEM((4, tok, quarter), BF16),
            pltpu.VMEM((4, rows, hidden), F32),
            pltpu.VMEM((2, 3, rows, hidden), BF16),
            pltpu.VMEM((4, 8 * tok, quarter), BF16),
            pltpu.VMEM((4, 4 * tok, quarter), BF16),
            pltpu.VMEM((4, 4 * tok, quarter), BF16),
            pltpu.VMEM((4, 4 * tok, quarter), BF16),
            pltpu.VMEM((4 * tok, quarter), BF16),
            pltpu.VMEM((4, tok, quarter), BF16),
            pltpu.VMEM((4, tok, quarter), BF16),
            pltpu.VMEM((rows, hidden), BF16),
            sems((2, 2, NC)), sems((2, 2, NC)), sems((2, 2, NC)), sems((2, 2, NC)),
            sems((NC,)), sems((2, NC)), sems((2, NC)), sems((2, NC)), sems((NC,)),
            sems((2, 2)), sems((2, 2)), sems((2,)), sems((2,)),
            *[sems((4,)) for _ in range(20)],
            sems((4,)),
        ],
        compiler_params=pltpu.CompilerParams(
            collective_id=0, has_side_effects=True, vmem_limit_bytes=56 * 2**20
        ),
        cost_estimate=pl.CostEstimate(
            flops=4 * 8 * tok * width * hidden, bytes_accessed=4 * 2**20, transcendentals=0
        ),
        name="backward",
    )(inputs, out_grad, weight)
    return pl.pallas_call(
        place,
        out_shape=(
            jax.ShapeDtypeStruct((tok, width), BF16),
            jax.ShapeDtypeStruct((rows, hidden), BF16),
        ),
        in_specs=[hbm] * 2,
        out_specs=(hbm, hbm),
        scratch_shapes=[
            pltpu.VMEM((tok, width), BF16), pltpu.VMEM((rows, hidden), BF16), sems((8,)), sems((8,)),
        ],
        name="place",
    )(parts, weight_grad)


def solution(mesh):
    return jax.shard_map(
        per_device,
        mesh=mesh,
        in_specs=(P(("dp", "gx", "gz"), "gy"), P(("dp", "gx", "gy"), "gz"), P(("gy", "gx"), "gz")),
        out_specs=(P(("dp", "gx", "gz"), "gy"), P(("gy", "gx"), "gz")),
        check_vma=False,
    )
```
